32 devices in a mesh: pop: 2 (over y), ctx: 4 (over z), exp: 2 (over x), tp: 2 (over core).
Axes of the slice: x: 2, y: 2, z: 4, core: 2. Of those that a mesh axis runs over, the one named last changes fastest.
Arguments:
- tokens: bfloat16 [2048, 2688], P(('pop', 'ctx', 'tp')), parts along dimension 0, may hold values from -6 to 6
- routes: int32 [2048, 6], P(('pop', 'ctx', 'tp')), parts along dimension 0, may hold values from 0 to 15, all different within a row; in each aligned block of 128 rows (0 to 127, 128 to 255, ...) at most 64 rows name the same one
- route_gates: float32 [2048, 6], P(('pop', 'ctx', 'tp')), parts along dimension 0, may hold values from 0.05 to 1
- up_weight: bfloat16 [16, 2688, 1536], P(('ctx', 'tp'), None, 'exp'), may hold values from -0.125 to 0.125
- down_weight: bfloat16 [16, 1536, 2688], P(('ctx', 'tp'), None, 'exp'), may hold values from -0.15625 to 0.15625
- factor_seeds: int32 [32, 4], P(('pop', 'ctx', 'tp')), parts along dimension 0, may hold values from 0 to 15
- up_left: bfloat16 [16, 2688], replicated, may hold values from -0.125 to 0.125
- up_right: bfloat16 [16, 1536], P(None, 'exp'), may hold values from -3 to 3
- down_left: bfloat16 [16, 1536], replicated, may hold values from -0.15625 to 0.15625
- down_right: bfloat16 [16, 2688], P(None, 'exp'), may hold values from -3 to 3
Outputs:
- moe_output: bfloat16 [2048, 2688], P(('pop', 'ctx', 'tp'), 'exp'), parts along dimension 0
The draws below stay inside these ranges and needn't reach their ends.
There are 2 independent parts, one for each index of `pop`. The reference program is written for one: setup_inputs(seed, part) draws one part's arguments, and reference() takes and returns one part's arrays. A program takes and returns all parts, laid end to end along the dimension named above; an argument that names none is the same for every part. Nothing has to cross between parts.
Inputs may be any that keep to these rules, and one draw needn't show every extreme that they name: `routes`: each row names 6 different experts. Among the 128 rows of one device (aligned blocks of 128 rows) no expert is named more than 64 times, and in every draw some expert is named exactly 64 times in some block.
All inputs are finite; a program needn't handle non-finite values.
Results may differ from the reference program's by a relative error of at most 0.0057.
Values may be sent and summed in bfloat16 or wider, within the bound.
No kernel may reach another device: no remote copies, remote signals or barrier semaphores. Data moves between devices by JAX's collectives and lax.ppermute only.
A program may use at most 64 MiB of HBM per device.

```python
import math
import jax
import jax.numpy as jnp
import numpy as np
from jax import lax

D = 2688
TOP = 6
HID = 1536
NFAC = 16
TOK_DEV = 128
EXPERTS = 16
CAP = 64
TOKENS = 1024
N_CTX = 4
N_TP = 2


def place_ends(result, key, smallest, largest):
    extent = result.shape
    spot = [jax.random.randint(jax.random.fold_in(key, axis), (), 0, extent[axis]) for axis in range(len(extent))]
    result = result.at[tuple(spot)].set(smallest)
    longest = extent.index(max(extent))
    spot[longest] = (spot[longest] + 1) % extent[longest]
    return result.at[tuple(spot)].set(largest)


def steps_of(stream_key, shape, shards, low, top_value):
    gain = 1.0
    for dim, blocks in shards:
        heights = jax.random.uniform(jax.random.fold_in(jax.random.fold_in(stream_key, 6), dim), (blocks,), jnp.float32, low / len(shards), top_value / len(shards))
        gain = gain * jnp.repeat(jnp.exp(heights), shape[dim] // blocks).reshape((-1,) + (1,) * (len(shape) - 1 - dim))
    return gain


def shared_out(own_key, own, number, rows, number_of, top, limit, lean):
    sequence = jax.random.permutation(own_key, number_of)
    heavy_load, common = portions_of(number_of, rows * top, limit, lean, True), portions_of(number_of, rows * top, limit, lean, False)
    places = jnp.arange(number_of)

    def named(tallies, turn):
        used = int((tallies > 0).sum())
        fixed = max(1, used // 4)
        passed = fixed + (places - fixed + turn * (used - fixed)) % max(1, number_of - fixed)
        return jnp.zeros((number_of,), jnp.int32).at[sequence[jnp.where(places < fixed, places, passed)]].set(jnp.asarray(tallies, jnp.int32))

    tallies = jnp.where(number % 4 == 0, named(heavy_load, number // 4), named(common, number - number // 4 - 1))
    mixed = jax.random.permutation(jax.random.fold_in(own, 3), number_of)
    giver, sink = mixed[0:number_of // 2 * 2:2], mixed[1:number_of // 2 * 2:2]
    slack = jnp.minimum(tallies[giver] - 1, limit - tallies[sink]) // 2
    slack = jnp.where((giver == sequence[0]) | (sink == sequence[0]) | (tallies[sink] == 0), 0, jnp.maximum(slack, 0))
    passed = jax.random.randint(jax.random.fold_in(own, 4), (number_of // 2,), 0, 1 << 20) % (slack + 1)
    tallies = tallies.at[giver].add(-passed).at[sink].add(passed)
    labels = jnp.searchsorted(jnp.cumsum(tallies), jnp.arange(rows * top), side="right").astype(jnp.int32)
    table = labels.reshape(top, rows).T
    table = table[jax.random.permutation(jax.random.fold_in(own, 1), rows)]
    turn = jax.random.randint(jax.random.fold_in(own, 2), (rows, 1), 0, top)
    return jnp.take_along_axis(table, (jnp.arange(top)[None, :] + turn) % top, axis=1)


def portions_of(number_of, total, most, lean, full):
    loads = [(1 << 20) // math.isqrt(rank ** lean) + 1 for rank in range(1, number_of + 1)]
    largest = most if full else min(most, max(-(-total // number_of), total * loads[0] // sum(loads)))
    least = 1 if total - largest >= number_of - 1 else 0
    given, rest = [largest] + [least] * (number_of - 1), total - largest - least * (number_of - 1)
    while rest > 0:
        free = [i for i in range(1, number_of) if given[i] < largest] or [i for i in range(1, number_of) if given[i] < most]
        whole, left = sum([loads[i] for i in free]), rest
        for i in free:
            extra = min(most - given[i], max(1, left * loads[i] // whole), rest)
            given[i] = given[i] + extra
            rest = rest - extra
    return np.array(given)


def noise(stream_key, extent, width, most, cuts=(), kind=jnp.bfloat16):
    factor_of = steps_of(stream_key, extent, cuts, -0.22, 0.18) if cuts else 1.0
    array = jax.random.normal(stream_key, extent, jnp.float32) * width * factor_of
    return jnp.minimum(jnp.maximum(array, -most), most).astype(kind)


def setup_inputs(seed: int = 0, part: int = 0) -> dict:
    seeds = jax.random.split(jax.random.key(seed), 11)
    part_keys = jax.random.split(jax.random.fold_in(seeds[10], part), 11)
    tokens = noise(part_keys[0], (TOKENS, D), 1.0, 6.0, ((0, 8),))
    routes_keys = jax.random.split(jax.random.fold_in(part_keys[1], 1), TOKENS // TOK_DEV)
    routes_turns = jax.random.permutation(jax.random.fold_in(part_keys[1], 3), TOKENS // TOK_DEV)
    routes = jax.vmap(lambda own, number: shared_out(jax.random.fold_in(part_keys[1], 2), own, number, TOK_DEV, EXPERTS, TOP, CAP, 2))(routes_keys, routes_turns).reshape((TOKENS, TOP))
    route_gates = jnp.clip(jnp.exp(math.log(1.0) - 2.9957323 * jax.random.uniform(part_keys[2], (TOKENS, TOP), jnp.float32) ** steps_of(part_keys[2], (TOKENS, TOP), ((0, 8),), -0.2, 0.2)), 0.05, 1.0)
    up_weight = noise(seeds[3], (EXPERTS, D, HID), D ** -0.5, 0.125, ((0, 8), (2, 2)))
    down_weight = noise(seeds[4], (EXPERTS, HID, D), HID ** -0.5, 0.15625, ((0, 8), (2, 2)))
    factor_seeds = place_ends(jax.random.randint(part_keys[5], (EXPERTS, 4), 0, NFAC), jax.random.fold_in(part_keys[5], 1), 0, NFAC - 1).astype(jnp.int32)
    up_left = noise(seeds[6], (NFAC, D), D ** -0.5, 0.125)
    up_right = noise(seeds[7], (NFAC, HID), 0.5, 3.0, ((1, 2),))
    down_left = noise(seeds[8], (NFAC, HID), HID ** -0.5, 0.15625)
    down_right = noise(seeds[9], (NFAC, D), 0.5, 3.0, ((1, 2),))
    return dict(tokens=tokens, routes=routes, route_gates=route_gates, up_weight=up_weight, down_weight=down_weight, factor_seeds=factor_seeds, up_left=up_left, up_right=up_right, down_left=down_left, down_right=down_right)


def reference(tokens, routes, route_gates, up_weight, down_weight, factor_seeds, up_left, up_right, down_left, down_right):
    flat_routes = routes.reshape(-1)
    normed = route_gates / jnp.sum(route_gates, axis=1, keepdims=True)
    flat_gates = normed.reshape(-1)
    slot_limit = N_CTX * N_TP * CAP

    def expert_step(summed, expert_id):
        ordering = jnp.argsort((flat_routes != expert_id).astype(jnp.int32), stable=True)[:slot_limit]
        is_live = flat_routes[ordering] == expert_id
        token_ids = (ordering // TOP).astype(jnp.int32)
        token_rows = tokens[token_ids]
        chosen = factor_seeds[expert_id]
        up_act = jnp.dot(token_rows, up_weight[expert_id], preferred_element_type=jnp.float32)
        low_rank = jnp.dot(token_rows, up_left[chosen[0]], preferred_element_type=jnp.float32)
        up_act = up_act + low_rank[:, None] * up_right[chosen[1]].astype(jnp.float32)
        hidden = (jnp.maximum(up_act, 0.0) ** 2).astype(jnp.bfloat16)
        down_act = jnp.dot(hidden, down_weight[expert_id], preferred_element_type=jnp.float32)
        down_rank = jnp.dot(hidden, down_left[chosen[2]], preferred_element_type=jnp.float32)
        down_act = down_act + down_rank[:, None] * down_right[chosen[3]].astype(jnp.float32)
        rounded = lax.optimization_barrier(down_act.astype(jnp.bfloat16))
        output = rounded.astype(jnp.float32)
        weight = jnp.where(is_live, flat_gates[ordering], jnp.zeros((), flat_gates.dtype))
        summed = summed.at[token_ids].add(weight[:, None] * output)
        return summed, None

    summed, _ = lax.scan(expert_step, jnp.zeros((TOKENS, D), jnp.float32), jnp.arange(EXPERTS, dtype=jnp.int32))
    return summed.astype(jnp.bfloat16)
```

```python
import functools

import jax
import jax.numpy as jnp
from jax import lax
from jax.experimental import pallas as pl
from jax.experimental.pallas import tpu as pltpu
from jax.sharding import PartitionSpec as P

LANES = 128
VMEM_LIMIT = 48 * 1024 * 1024


def shift(value, axis, by):
    size = lax.axis_size(axis)
    return lax.ppermute(value, axis, [(i, (i + by) % size) for i in range(size)])


def iota(shape, dim):
    return lax.broadcasted_iota(jnp.int32, shape, dim)


def prep_kernel(experts_all, parts, scalars, tokens, routes, gates, up_left, *refs):
    pieces, info = refs[:-1], refs[-1]
    count, model_width = tokens.shape
    width = info.shape[1]
    factors = up_left.shape[0]
    rows = count // parts
    lane = iota((count, width), 1)
    expert = lax.rem(lane, experts_all)
    gate_all = gates[...]
    normed = gate_all / jnp.sum(gate_all, axis=1, keepdims=True)
    named = jnp.zeros((count, width), jnp.float32)
    gate = jnp.zeros((count, width), jnp.float32)
    for k in range(routes.shape[1]):
        hit = routes[:, k : k + 1] == expert
        named = jnp.where(hit, 1.0, named)
        gate = jnp.where(hit, normed[:, k : k + 1], gate)
    before = (iota((count, count), 1) < iota((count, count), 0)).astype(jnp.bfloat16)
    slot = jnp.dot(before, named.astype(jnp.bfloat16), preferred_element_type=jnp.float32)
    slot = jnp.where(named > 0.0, slot, -1.0)
    row = iota((width, factors), 0) - 3 * experts_all
    pick = (row >= 0) & (row < 2 * factors) & (lax.rem(row, factors) == iota((width, factors), 1))
    left = jnp.dot(
        pick.astype(jnp.bfloat16), up_left[...], preferred_element_type=jnp.float32
    ).astype(jnp.bfloat16)
    low_rank = lax.dot_general(
        tokens[...], left, (((1,), (1,)), ((), ())), preferred_element_type=jnp.float32
    )
    value = jnp.where(lane < 3 * experts_all, gate, low_rank)
    high = value.astype(jnp.bfloat16).astype(jnp.float32)
    is_low = ((lane >= 2 * experts_all) & (lane < 3 * experts_all)) | (
        lane >= 3 * experts_all + factors
    )
    value = jnp.where(is_low, value - high, high)
    info[...] = jnp.where(lane < experts_all, slot, value).astype(jnp.bfloat16)
    for j, piece in enumerate(pieces):
        at = pl.multiple_of(lax.rem(scalars[0] - j + parts, parts) * rows, rows)
        piece[:, :model_width] = tokens[pl.ds(at, rows), :]
        piece[:, model_width:] = info[pl.ds(at, rows), :]


def up_kernel(
    experts_all, parts, cores, capacity, factors, scalars, *refs
):
    pieces = refs[: parts * cores]
    weight, right, hidden, gate_out, block, slots = refs[parts * cores :]
    rows = pieces[0].shape[0]
    tok_count = rows * parts
    model_width = weight.shape[1]
    width = block.shape[1] - model_width
    local_experts = slots.shape[0]
    slot_count = local_experts * capacity
    local = pl.program_id(0)

    @pl.when((local == 0) & (pl.program_id(1) == 0))
    def dispatch():
        column = iota((width, 2 * slot_count), 0)
        slot = iota((width, 2 * slot_count), 1)
        owner = scalars[1] + lax.rem(slot, slot_count) // capacity
        place_of = (column == owner).astype(jnp.bfloat16)
        gate_of = (
            column == owner + jnp.where(slot < slot_count, experts_all, 2 * experts_all)
        ).astype(jnp.bfloat16)
        wanted = lax.rem(iota((tok_count, 2 * slot_count), 1), capacity).astype(jnp.float32)
        for b in range(cores):
            for j in range(parts):
                block[j * rows : (j + 1) * rows, :] = pieces[b * parts + j][...]
            info = block[:, model_width:]
            place = jnp.dot(info, place_of, preferred_element_type=jnp.float32)
            gate = jnp.dot(info, gate_of, preferred_element_type=jnp.float32)
            here = place == wanted
            gate = jnp.where(here, gate, 0.0).astype(jnp.bfloat16)
            for j in range(parts):
                at = pl.multiple_of(lax.rem(scalars[0] - j + parts, parts) * rows, rows)
                gate_out[b, pl.ds(at, rows), :] = gate[j * rows : (j + 1) * rows, :]
            chooser = here[:, :slot_count].astype(jnp.bfloat16)
            chosen = lax.dot_general(
                chooser, block[...], (((0,), (0,)), ((), ())), preferred_element_type=jnp.float32
            ).astype(jnp.bfloat16)
            for l in range(local_experts):
                slots[l, b * capacity : (b + 1) * capacity, :] = chosen[
                    l * capacity : (l + 1) * capacity, :
                ]

    seed_left, seed_right = scalars[2 + 4 * local], scalars[3 + 4 * local]
    extra = slots[local, :, model_width:].astype(jnp.float32)
    lane = iota(extra.shape, 1) - 3 * experts_all
    low_rank = jnp.sum(
        jnp.where((lane == seed_left) | (lane == factors + seed_left), extra, 0.0),
        axis=1,
        keepdims=True,
    )
    table = right[...].astype(jnp.float32)
    right_row = jnp.sum(
        jnp.where(iota(table.shape, 0) == seed_right, table, 0.0), axis=0, keepdims=True
    )
    up_act = jnp.dot(
        slots[local, :, :model_width], weight[0], preferred_element_type=jnp.float32
    )
    up_act = jnp.maximum(up_act + low_rank * right_row, 0.0)
    hidden[0] = (up_act * up_act).astype(jnp.bfloat16)


def down_kernel(parts, cores, capacity, scalars, *refs):
    hiddens = refs[:parts]
    weight, left, right, gate, own, others, total, rank, results = refs[parts:]
    local, part = pl.program_id(0), pl.program_id(1)
    local_experts = pl.num_programs(0)
    slot_count = results.shape[1] // 2
    seed_left, seed_right = scalars[4 + 4 * local], scalars[5 + 4 * local]
    left_table = left[0].astype(jnp.float32)
    left_row = jnp.sum(
        jnp.where(iota(left_table.shape, 0) == seed_left, left_table, 0.0), axis=0, keepdims=True
    )
    for j in range(parts):

        @pl.when(part == j)
        def add(j=j):
            value = hiddens[j][0]
            product = jnp.dot(value, weight[0], preferred_element_type=jnp.float32)
            low_rank = jnp.sum(value.astype(jnp.float32) * left_row, axis=1, keepdims=True)
            if j:
                product = product + total[...]
                low_rank = low_rank + rank[:, :1]
            if j < parts - 1:
                total[...] = product
                rank[...] = jnp.broadcast_to(low_rank, rank.shape)
            else:
                table = right[...].astype(jnp.float32)
                right_row = jnp.sum(
                    jnp.where(iota(table.shape, 0) == seed_right, table, 0.0),
                    axis=0,
                    keepdims=True,
                )
                result = (product + low_rank * right_row).astype(jnp.bfloat16)
                for b in range(cores):
                    for half in range(2):
                        at = pl.multiple_of(half * slot_count + local * capacity, capacity)
                        results[b, pl.ds(at, capacity), :] = result[
                            b * capacity : (b + 1) * capacity, :
                        ]

    @pl.when((local == local_experts - 1) & (part == parts - 1))
    def combine():
        for b in range(cores):
            summed = jnp.dot(gate[b], results[b], preferred_element_type=jnp.float32)
            if b == 0:
                own[...] = summed
            else:
                others[b - 1] = summed.astype(jnp.bfloat16)


def on_device(
    tokens,
    routes,
    route_gates,
    up_weight,
    down_weight,
    factor_seeds,
    up_left,
    up_right,
    down_left,
    down_right,
):
    chips, cores, parts = lax.axis_size("ctx"), lax.axis_size("tp"), lax.axis_size("exp")
    local_experts, model_width, hid = up_weight.shape
    out_width = down_weight.shape[2]
    experts_all = chips * cores * local_experts
    tok_count, top_count = routes.shape
    factors = up_left.shape[0]
    capacity = 4 * tok_count * top_count // (3 * experts_all)
    rows = tok_count // parts
    width = -(-(3 * experts_all + 2 * factors) // LANES) * LANES
    packed = model_width + width
    slot_count = local_experts * capacity
    expert_rows = cores * capacity
    first_expert = (lax.axis_index("ctx") * cores + lax.axis_index("tp")) * local_experts
    scalars = jnp.concatenate(
        [
            jnp.stack([lax.axis_index("exp"), first_expert]).astype(jnp.int32),
            factor_seeds.reshape(-1),
        ]
    )
    left_parts = down_left.reshape(factors, parts, hid).transpose(1, 0, 2)
    params = pltpu.CompilerParams(vmem_limit_bytes=VMEM_LIMIT)

    prep = pl.pallas_call(
        functools.partial(prep_kernel, experts_all, parts),
        out_shape=[jax.ShapeDtypeStruct((rows, packed), jnp.bfloat16)] * parts,
        grid_spec=pltpu.PrefetchScalarGridSpec(
            num_scalar_prefetch=1,
            grid=(1,),
            in_specs=[
                pl.BlockSpec(shape, lambda i, s: (0, 0))
                for shape in (tokens.shape, routes.shape, routes.shape, up_left.shape)
            ],
            out_specs=[pl.BlockSpec((rows, packed), lambda i, s: (0, 0))] * parts,
            scratch_shapes=[pltpu.VMEM((tok_count, width), jnp.bfloat16)],
        ),
        compiler_params=params,
        name="pack_tokens",
    )

    up_tile = 2 * LANES if hid % (2 * LANES) == 0 else hid
    up = pl.pallas_call(
        functools.partial(up_kernel, experts_all, parts, cores, capacity, factors),
        out_shape=[
            jax.ShapeDtypeStruct((local_experts, expert_rows, hid), jnp.bfloat16),
            jax.ShapeDtypeStruct((cores, tok_count, 2 * slot_count), jnp.bfloat16),
        ],
        grid_spec=pltpu.PrefetchScalarGridSpec(
            num_scalar_prefetch=1,
            grid=(local_experts, hid // up_tile),
            in_specs=[pl.BlockSpec((rows, packed), lambda l, n, s: (0, 0))] * (parts * cores)
            + [
                pl.BlockSpec((1, model_width, up_tile), lambda l, n, s: (l, 0, n)),
                pl.BlockSpec((factors, up_tile), lambda l, n, s: (0, n)),
            ],
            out_specs=[
                pl.BlockSpec((1, expert_rows, up_tile), lambda l, n, s: (l, 0, n)),
                pl.BlockSpec((cores, tok_count, 2 * slot_count), lambda l, n, s: (0, 0, 0)),
            ],
            scratch_shapes=[
                pltpu.VMEM((tok_count, packed), jnp.bfloat16),
                pltpu.VMEM((local_experts, expert_rows, packed), jnp.bfloat16),
            ],
        ),
        compiler_params=params,
        cost_estimate=pl.CostEstimate(
            flops=2 * slot_count * cores * model_width * hid,
            bytes_accessed=2 * up_weight.size,
            transcendentals=0,
        ),
        name="up",
    )

    def turned(j, s):
        return lax.rem(s[0] - j + parts, parts)

    down = pl.pallas_call(
        functools.partial(down_kernel, parts, cores, capacity),
        out_shape=[
            jax.ShapeDtypeStruct((tok_count, out_width), jnp.float32),
            jax.ShapeDtypeStruct((cores - 1, tok_count, out_width), jnp.bfloat16),
        ],
        grid_spec=pltpu.PrefetchScalarGridSpec(
            num_scalar_prefetch=1,
            grid=(local_experts, parts),
            in_specs=[pl.BlockSpec((1, expert_rows, hid), lambda l, j, s: (l, 0, 0))] * parts
            + [
                pl.BlockSpec((1, hid, out_width), lambda l, j, s: (l, turned(j, s), 0)),
                pl.BlockSpec((1, factors, hid), lambda l, j, s: (turned(j, s), 0, 0)),
                pl.BlockSpec((factors, out_width), lambda l, j, s: (0, 0)),
                pl.BlockSpec((cores, tok_count, 2 * slot_count), lambda l, j, s: (0, 0, 0)),
            ],
            out_specs=[
                pl.BlockSpec((tok_count, out_width), lambda l, j, s: (0, 0)),
                pl.BlockSpec((cores - 1, tok_count, out_width), lambda l, j, s: (0, 0, 0)),
            ],
            scratch_shapes=[
                pltpu.VMEM((expert_rows, out_width), jnp.float32),
                pltpu.VMEM((expert_rows, LANES), jnp.float32),
                pltpu.VMEM((cores, 2 * slot_count, out_width), jnp.bfloat16),
            ],
        ),
        compiler_params=params,
        cost_estimate=pl.CostEstimate(
            flops=2 * slot_count * cores * parts * hid * out_width,
            bytes_accessed=2 * down_weight.size,
            transcendentals=0,
        ),
        name="down",
    )

    own_pieces = list(prep(scalars, tokens, routes, route_gates, up_left))

    def compute(pieces):
        blocks = list(pieces)
        for b in range(1, cores):
            blocks += [shift(piece, "tp", b) for piece in pieces]
        hidden, gate = up(scalars, *blocks, up_weight, up_right)
        hiddens = [hidden] + [shift(hidden, "exp", j) for j in range(1, parts)]
        own, others = down(scalars, *hiddens, down_weight, left_parts, down_right, gate)
        return own, [shift(others[b - 1], "tp", -b) for b in range(1, cores)]

    sums = [compute(own_pieces)]
    travelling = own_pieces[0]
    for _ in range(1, chips):
        travelling = shift(travelling, "ctx", 1)
        pieces = [travelling] + [shift(travelling, "exp", j) for j in range(1, parts)]
        sums.append(compute(pieces))
    carried = None
    for own, swapped in sums[1:] + sums[:1]:
        total = own
        for value in swapped + ([carried] if carried is not None else []):
            total = total + value.astype(jnp.float32)
        total = total.astype(jnp.bfloat16)
        if own is not sums[0][0]:
            carried = shift(total, "ctx", 1)
    return total


def solution(mesh):
    in_specs = (
        P(("pop", "ctx", "tp"), None),
        P(("pop", "ctx", "tp"), None),
        P(("pop", "ctx", "tp"), None),
        P(("ctx", "tp"), None, "exp"),
        P(("ctx", "tp"), None, "exp"),
        P(("pop", "ctx", "tp"), None),
        P(),
        P(None, "exp"),
        P(),
        P(None, "exp"),
    )
    out_specs = P(("pop", "ctx", "tp"), "exp")
    return jax.shard_map(
        on_device, mesh=mesh, in_specs=in_specs, out_specs=out_specs, check_vma=False
    )
```

```python
import functools

import jax
import jax.numpy as jnp
from jax import lax
from jax.experimental import pallas as pl
from jax.experimental.pallas import tpu as pltpu
from jax.sharding import PartitionSpec as P

LANES = 128
VMEM_LIMIT = 24 * 1024 * 1024
NT = (((1,), (1,)), ((), ()))
TN = (((0,), (0,)), ((), ()))


def shift(value, axis, by):
    size = lax.axis_size(axis)
    return lax.ppermute(value, axis, [(i, (i + by) % size) for i in range(size)])


in_memory = pltpu.with_memory_space_constraint


def after(value, earlier):
    return lax.optimization_barrier((value, earlier))[0]


def iota(shape, dim):
    return lax.broadcasted_iota(jnp.int32, shape, dim)


def prep_kernel(experts_all, parts, place, routes, gates, tokens, up_left, *refs):
    pieces, (routes_in, gates_in, rows_in, table_in, info, sems) = refs[:parts], refs[parts:]
    count, model_width = tokens.shape
    width = info.shape[1]
    factors = up_left.shape[0]
    rows = count // parts
    copies = [
        pltpu.make_async_copy(source, target, sems.at[i])
        for i, (source, target) in enumerate(
            ((routes, routes_in), (gates, gates_in), (up_left, table_in), (tokens, rows_in))
        )
    ]
    for copy in copies:
        copy.start()
    line = iota((width, count), 0)
    expert = lax.rem(line, experts_all)
    after_it = (iota((count, count), 0) < iota((count, count), 1)).astype(jnp.bfloat16)
    row = iota((width, factors), 0) - 3 * experts_all
    pick = (row >= 0) & (row < 2 * factors) & (lax.rem(row, factors) == iota((width, factors), 1))
    for copy in copies[:2]:
        copy.wait()
    gate_all = gates_in[...]
    normed = gate_all / jnp.sum(gate_all, axis=0, keepdims=True)
    named = jnp.zeros((width, count), jnp.float32)
    gate = jnp.zeros((width, count), jnp.float32)
    for k in range(routes.shape[0]):
        hit = routes_in[k : k + 1, :] == expert
        named = jnp.where(hit, 1.0, named)
        gate = jnp.where(hit, normed[k : k + 1, :], gate)
    slot = jnp.dot(named.astype(jnp.bfloat16), after_it, preferred_element_type=jnp.float32)
    slot = jnp.where(named > 0.0, slot, -1.0)
    copies[2].wait()
    left = jnp.dot(
        pick.astype(jnp.bfloat16), table_in[...], preferred_element_type=jnp.float32
    ).astype(jnp.bfloat16)
    copies[3].wait()
    low_rank = lax.dot_general(left, rows_in[...], NT, preferred_element_type=jnp.float32)
    value = jnp.where(line < 3 * experts_all, gate, low_rank)
    high = value.astype(jnp.bfloat16).astype(jnp.float32)
    is_low = ((line >= 2 * experts_all) & (line < 3 * experts_all)) | (
        line >= 3 * experts_all + factors
    )
    value = jnp.where(is_low, value - high, high)
    info[...] = jnp.where(line < experts_all, slot, value).T.astype(jnp.bfloat16)
    for j, piece in enumerate(pieces):
        at = pl.multiple_of(lax.rem(place[0] - j + parts, parts) * rows, rows)
        piece[:, :model_width] = rows_in[pl.ds(at, rows), :]
        piece[:, model_width:] = info[pl.ds(at, rows), :]


def up_kernel(first, experts_all, parts, cores, splits, capacity, factors, place, seeds, *refs):
    count = parts * (1 + (cores - 1) * splits)
    pieces = refs[:count]
    weight, right, hidden, gate_out, *tiles, block, slots, right_in, sems = refs[count:]
    rows = pieces[0].shape[0]
    tok_count = rows * parts
    tiles = tiles[0] if first else weight
    local_experts, _, hid = hidden.shape
    steps = tiles.shape[0] // local_experts
    model_width, tile = tiles.shape[1:]
    width = block.shape[1] - model_width
    expert_rows = cores * capacity
    slot_count = local_experts * expert_rows

    right_copy = pltpu.make_async_copy(right, right_in, sems.at[0])
    right_copy.start()
    copies = []
    if first:
        copies = [
            pltpu.make_async_copy(
                weight.at[l, :, pl.ds(n * tile, tile)],
                tiles.at[l * steps + n],
                sems.at[1 + l * steps + n],
            )
            for l in range(local_experts)
            for n in range(steps)
        ]
    for copy in copies:
        copy.start()

    column = iota((width, 2 * slot_count), 0)
    slot = iota((width, 2 * slot_count), 1)
    owner = place[1] + lax.rem(slot, slot_count) // expert_rows
    place_of = (column == owner).astype(jnp.bfloat16)
    gate_of = (
        column == owner + jnp.where(slot < slot_count, experts_all, 2 * experts_all)
    ).astype(jnp.bfloat16)
    lane = iota((tok_count, 2 * slot_count), 1)
    wanted = lax.rem(lane, capacity).astype(jnp.float32)
    base = 0
    for piece in pieces:
        block[base : base + piece.shape[0], :] = piece[...]
        base += piece.shape[0]
    choosers = []
    for b in range(cores):
        base = b * tok_count
        info = block[base : base + tok_count, model_width:]
        slot_of = jnp.dot(info, place_of, preferred_element_type=jnp.float32)
        gate = jnp.dot(info, gate_of, preferred_element_type=jnp.float32)
        here = (slot_of == wanted) & (lax.rem(lane, expert_rows) // capacity == b)
        gate = jnp.where(here, gate, 0.0).astype(jnp.bfloat16)
        for j in range(parts):
            at = lax.rem(place[0] - j + parts, parts) * rows
            gate_out[pl.ds(pl.multiple_of(base + at, rows), rows), :] = gate[
                j * rows : (j + 1) * rows, :
            ]
        choosers.append(here[:, :slot_count].astype(jnp.bfloat16))
    slots[...] = lax.dot_general(
        jnp.concatenate(choosers, axis=0), block[...], TN, preferred_element_type=jnp.float32
    ).astype(jnp.bfloat16)

    right_copy.wait()
    table = right_in[...].astype(jnp.float32)
    for l in range(local_experts):
        mine = slice(l * expert_rows, (l + 1) * expert_rows)
        extra = slots[mine, model_width:].astype(jnp.float32)
        at = iota(extra.shape, 1) - 3 * experts_all
        low_rank = jnp.sum(
            jnp.where((at == seeds[l, 0]) | (at == factors + seeds[l, 0]), extra, 0.0),
            axis=1,
            keepdims=True,
        )
        right_row = jnp.sum(
            jnp.where(iota(table.shape, 0) == seeds[l, 1], table, 0.0), axis=0, keepdims=True
        )
        for n in range(steps):
            if first:
                copies[l * steps + n].wait()
            up_act = jnp.dot(
                slots[mine, :model_width],
                tiles[l * steps + n],
                preferred_element_type=jnp.float32,
            )
            here = slice(n * tile, (n + 1) * tile)
            up_act = jnp.maximum(up_act + low_rank * right_row[:, here], 0.0)
            hidden[l, :, here] = (up_act * up_act).astype(jnp.bfloat16)


def down_kernel(first, parts, cores, pieces_out, place, seeds, *refs):
    pieces = refs[:parts]
    weight, left, right, gate, own, *rest = refs[parts:]
    others, rest = rest[: (cores - 1) * pieces_out], rest[(cores - 1) * pieces_out :]
    *tiles, results, left_in, right_in, sems = rest
    tiles = tiles[0] if first else weight
    local_experts, expert_rows, depth = pieces[0].shape
    steps = tiles.shape[0] // local_experts
    tile = tiles.shape[1]
    slot_count = local_experts * expert_rows
    tok_count = gate.shape[0] // cores

    tables = [
        pltpu.make_async_copy(left, left_in, sems.at[0]),
        pltpu.make_async_copy(right, right_in, sems.at[1]),
    ]
    copies = []
    if first:
        copies = [
            pltpu.make_async_copy(
                weight.at[l, pl.ds(n * tile, tile), :],
                tiles.at[l * steps + n],
                sems.at[2 + l * steps + n],
            )
            for l in range(local_experts)
            for n in range(steps)
        ]
    for copy in tables + copies:
        copy.start()

    columns = [slice(None)]
    if parts > 1:
        columns = [
            pl.ds(pl.multiple_of(lax.rem(place[0] - j + parts, parts) * depth, depth), depth)
            for j in range(parts)
        ]
    for copy in tables:
        copy.wait()
    for l in range(local_experts):
        rank_all = sum(
            lax.dot_general(left_in[:, at], piece[l], NT, preferred_element_type=jnp.float32)
            for at, piece in zip(columns, pieces)
        )
        rank = jnp.sum(
            jnp.where(iota(rank_all.shape, 0) == seeds[l, 2], rank_all, 0.0),
            axis=0,
            keepdims=True,
        )
        chosen = (iota((right.shape[0], expert_rows), 0) == seeds[l, 3]).astype(jnp.bfloat16)
        for n in range(steps):
            if first:
                copies[l * steps + n].wait()
            result = sum(
                lax.dot_general(
                    tiles[l * steps + n, :, at], piece[l], NT, preferred_element_type=jnp.float32
                )
                for at, piece in zip(columns, pieces)
            )
            here = slice(n * tile, (n + 1) * tile)
            right_column = lax.dot_general(
                right_in[:, here], chosen, TN, preferred_element_type=jnp.float32
            )
            result = (result + right_column * rank).astype(jnp.bfloat16)
            for half in range(2):
                at = half * slot_count + l * expert_rows
                results[here, at : at + expert_rows] = result
    summed = lax.dot_general(results[...], gate[...], NT, preferred_element_type=jnp.float32)
    own[...] = summed[:, :tok_count]
    step = summed.shape[0] // pieces_out
    for b in range(1, cores):
        for i in range(pieces_out):
            others[(b - 1) * pieces_out + i][...] = summed[
                i * step : (i + 1) * step, b * tok_count : (b + 1) * tok_count
            ].astype(jnp.bfloat16)


def on_device(
    tokens,
    routes,
    route_gates,
    up_weight,
    down_weight,
    factor_seeds,
    up_left,
    up_right,
    down_left,
    down_right,
):
    chips, cores, parts = lax.axis_size("ctx"), lax.axis_size("tp"), lax.axis_size("exp")
    local_experts, model_width, hid = up_weight.shape
    hid_all, out_width = down_weight.shape[1:]
    experts_all = chips * cores * local_experts
    tok_count, top_count = routes.shape
    factors = up_left.shape[0]
    capacity = 4 * tok_count * top_count // (3 * experts_all)
    rows = tok_count // parts
    width = -(-(3 * experts_all + 2 * factors) // LANES) * LANES
    packed = model_width + width
    expert_rows = cores * capacity
    slot_count = local_experts * expert_rows
    all_tokens = cores * tok_count
    first_expert = (lax.axis_index("ctx") * cores + lax.axis_index("tp")) * local_experts
    place = jnp.stack([lax.axis_index("exp"), first_expert]).astype(jnp.int32)
    whole_tiles = hid % LANES == 0
    params = pltpu.CompilerParams(vmem_limit_bytes=VMEM_LIMIT)
    smem, vmem, hbm = (
        pl.BlockSpec(memory_space=space) for space in (pltpu.SMEM, pltpu.VMEM, pltpu.HBM)
    )

    prep = pl.pallas_call(
        functools.partial(prep_kernel, experts_all, parts),
        out_shape=[jax.ShapeDtypeStruct((rows, packed), jnp.bfloat16)] * parts,
        in_specs=[smem, hbm, hbm, hbm, hbm],
        out_specs=[vmem] * parts,
        scratch_shapes=[
            pltpu.VMEM((top_count, tok_count), jnp.int32),
            pltpu.VMEM((top_count, tok_count), jnp.float32),
            pltpu.VMEM(tokens.shape, jnp.bfloat16),
            pltpu.VMEM(up_left.shape, jnp.bfloat16),
            pltpu.VMEM((tok_count, width), jnp.bfloat16),
            pltpu.SemaphoreType.DMA((4,)),
        ],
        compiler_params=params,
        name="pack_tokens",
    )

    splits = 2 if rows % 32 == 0 else 1
    up_steps = 3 if hid % (3 * LANES) == 0 else 1
    up_tiles = (local_experts * up_steps, model_width, hid // up_steps)

    def up(first):
        return pl.pallas_call(
            functools.partial(
                up_kernel, first, experts_all, parts, cores, splits, capacity, factors
            ),
            out_shape=[
                jax.ShapeDtypeStruct((local_experts, expert_rows, hid), jnp.bfloat16),
                jax.ShapeDtypeStruct((all_tokens, 2 * slot_count), jnp.bfloat16),
            ]
            + [jax.ShapeDtypeStruct(up_tiles, jnp.bfloat16)] * first,
            in_specs=[smem, smem] + [vmem] * (parts * (1 + (cores - 1) * splits)) + [hbm if first else vmem, hbm],
            out_specs=[vmem] * (2 + first),
            scratch_shapes=[
                pltpu.VMEM((all_tokens, packed), jnp.bfloat16),
                pltpu.VMEM((slot_count, packed), jnp.bfloat16),
                pltpu.VMEM(up_right.shape, jnp.bfloat16),
                pltpu.SemaphoreType.DMA((1 + local_experts * up_steps,)),
            ],
            compiler_params=params,
            name="up",
        )

    r_splits = 2 if out_width % 64 == 0 else 1
    down_steps = 3 if out_width % 48 == 0 else 1
    down_tiles = (local_experts * down_steps, out_width // down_steps, hid_all)
    hidden_parts = parts if whole_tiles else 1

    def down(first):
        return pl.pallas_call(
            functools.partial(down_kernel, first, hidden_parts, cores, r_splits),
            out_shape=[
                jax.ShapeDtypeStruct((out_width, tok_count), jnp.float32),
            ]
            + [jax.ShapeDtypeStruct((out_width // r_splits, tok_count), jnp.bfloat16)]
            * ((cores - 1) * r_splits)
            + [jax.ShapeDtypeStruct(down_tiles, jnp.bfloat16)] * first,
            in_specs=[smem, smem]
            + [vmem] * hidden_parts
            + [hbm if first else vmem, hbm, hbm, vmem],
            out_specs=[vmem] * (1 + (cores - 1) * r_splits + first),
            scratch_shapes=[
                pltpu.VMEM((out_width, 2 * slot_count), jnp.bfloat16),
                pltpu.VMEM(down_left.shape, jnp.bfloat16),
                pltpu.VMEM(down_right.shape, jnp.bfloat16),
                pltpu.SemaphoreType.DMA((2 + local_experts * down_steps,)),
            ],
            compiler_params=params,
            name="down",
        )

    place = in_memory(place, pltpu.SMEM)
    seeds = in_memory(factor_seeds, pltpu.SMEM)
    in_hbm = [
        in_memory(value, pltpu.HBM)
        for value in (
            routes.T, route_gates.T, tokens, up_left, up_weight, up_right,
            down_weight.transpose(0, 2, 1), down_left, down_right,
        )
    ]
    up_weight, up_right, down_turned, down_left, down_right = in_hbm[4:]
    pieces = list(prep(place, *in_hbm[:4]))
    kept = {}

    last = [pieces[0]]

    def order(value):
        last[0] = after(value, last[0])
        return last[0]

    def over_cores(piece):
        step = rows // splits
        return [
            [shift(piece[i * step : (i + 1) * step], "tp", b) for i in range(splits)]
            for b in range(1, cores)
        ]

    def over_exp(value):
        return [shift(value, "exp", j) for j in range(1, parts)]

    def run_up(here, there):
        blocks = here + [
            there[j][b][i] for b in range(cores - 1) for j in range(parts) for i in range(splits)
        ]
        first = "up" not in kept
        hidden, gate, *tiles = up(first)(
            place, seeds, order(blocks[0]), *blocks[1:], up_weight if first else kept["up"], up_right
        )
        if first:
            kept["up"] = tiles[0]
        last[0] = gate
        if whole_tiles:
            return [hidden] + over_exp(hidden), gate
        return [lax.all_gather(hidden, "exp", axis=2, tiled=True)], gate

    def run_down(hiddens, gate):
        first = "down" not in kept
        own, *others = down(first)(
            place,
            seeds,
            *hiddens[:-1],
            order(hiddens[-1]),
            down_turned if first else kept["down"],
            down_left,
            down_right,
            gate,
        )
        if first:
            kept["down"] = others.pop()
        last[0] = own
        return own, others

    def back(others):
        return [
            [shift(others[(b - 1) * r_splits + i], "tp", -b) for i in range(r_splits)]
            for b in range(1, cores)
        ]

    def add(own, swapped, *values):
        arrays = [piece for pieces in swapped for piece in pieces]

        def kernel(own, *refs):
            out, refs = refs[-1], refs[:-1]
            step = own.shape[0] // r_splits
            for i in range(r_splits):
                at = slice(i * step, (i + 1) * step)
                total = own[at, :]
                for b in range(cores - 1):
                    total = total + refs[b * r_splits + i][...].astype(jnp.float32)
                for value in refs[len(arrays) :]:
                    total = total + value[at, :].astype(jnp.float32)
                out[at, :] = total.astype(jnp.bfloat16)

        return pl.pallas_call(
            kernel,
            out_shape=jax.ShapeDtypeStruct(own.shape, jnp.bfloat16),
            in_specs=[vmem] * (1 + len(arrays) + len(values)),
            out_specs=vmem,
            compiler_params=params,
            cost_estimate=pl.CostEstimate(flops=1, bytes_accessed=1, transcendentals=0),
            name="add",
        )(own, *arrays, *values)

    def summed(own, others, *more):
        return add(own, back(others), *more)

    returned = {}

    def give_back(k, own, others):
        total = order(summed(own, [after(others[0], last[0])] + others[1:], *([returned[k - 1]] if k > 2 else [])))
        returned[k] = shift(total, "ctx", -1 if k == 1 else 1)

    arriving = shift(pieces[0], "ctx", 1)
    direct = [shift(piece, "ctx", -1) for piece in pieces[1:]]
    work = [run_up(pieces, [over_cores(piece) for piece in pieces])]
    arriving = order(arriving)
    direct = [order(piece) for piece in direct]
    direct_there = [over_cores(piece) for piece in direct]
    for k in range(1, chips):
        here = [arriving] + (over_exp(arriving) if k < chips - 1 else direct)
        there = [over_cores(arriving)]
        if k < chips - 1:
            arriving = shift(arriving, "ctx", 1)
        if k == 1:
            own_sum, own_others = run_down(*work[0])
            arriving = order(arriving)
        if k < chips - 1:
            here[1:] = [order(piece) for piece in here[1:]]
            there += [over_cores(piece) for piece in here[1:]]
        else:
            there += direct_there
        work.append(run_up(here, there))
        if 1 < k < chips - 1:
            arriving = order(arriving)
    for k in range(1, chips):
        sums = run_down(*work[k])
        give_back(k, *sums)
        if 1 < k == chips - 2:
            returned[1] = order(returned[1])
    homeward = {1, chips - 1}
    return add(own_sum, back(own_others), *(returned[k] for k in sorted(homeward))).T


def solution(mesh):
    in_specs = (
        P(("pop", "ctx", "tp"), None),
        P(("pop", "ctx", "tp"), None),
        P(("pop", "ctx", "tp"), None),
        P(("ctx", "tp"), None, "exp"),
        P(("ctx", "tp"), None, "exp"),
        P(("pop", "ctx", "tp"), None),
        P(),
        P(None, "exp"),
        P(),
        P(None, "exp"),
    )
    out_specs = P(("pop", "ctx", "tp"), "exp")
    return jax.shard_map(
        on_device, mesh=mesh, in_specs=in_specs, out_specs=out_specs, check_vma=False
    )
```

```python
import functools

import jax
import jax.numpy as jnp
from jax import lax
from jax.experimental import pallas as pl
from jax.experimental.pallas import tpu as pltpu
from jax.sharding import PartitionSpec as P

LANES = 128
VMEM_LIMIT = 24 * 1024 * 1024
NT = (((1,), (1,)), ((), ()))
TN = (((0,), (0,)), ((), ()))


def shift(value, axis, by):
    size = lax.axis_size(axis)
    return lax.ppermute(value, axis, [(i, (i + by) % size) for i in range(size)])


in_memory = pltpu.with_memory_space_constraint


def after(value, earlier):
    return lax.optimization_barrier((value, earlier))[0]


def iota(shape, dim):
    return lax.broadcasted_iota(jnp.int32, shape, dim)


def my_part():
    return lax.axis_index("exp")


def first_expert(local_experts):
    return (lax.axis_index("ctx") * lax.axis_size("tp") + lax.axis_index("tp")) * local_experts


def prep_kernel(experts_all, parts, routes, gates, tokens, up_left, weight, *refs):
    pieces, tiles = refs[:parts], refs[parts]
    routes_in, gates_in, rows_in, table_in, info, sems = refs[parts + 1 :]
    count, model_width = tokens.shape
    width = info.shape[1]
    factors = up_left.shape[0]
    rows = count // parts
    copies = [
        pltpu.make_async_copy(source, target, sems.at[i])
        for i, (source, target) in enumerate(
            ((routes, routes_in), (gates, gates_in), (up_left, table_in), (tokens, rows_in))
        )
    ]
    steps, _, tile = tiles.shape
    loads = [
        pltpu.make_async_copy(
            weight.at[0, :, pl.ds(n * tile, tile)], tiles.at[n], sems.at[len(copies) + n]
        )
        for n in range(steps)
    ]
    for copy in copies + loads:
        copy.start()
    line = iota((width, count), 0)
    expert = lax.rem(line, experts_all)
    after_it = (iota((count, count), 0) < iota((count, count), 1)).astype(jnp.bfloat16)
    row = iota((width, factors), 0) - 3 * experts_all
    pick = (row >= 0) & (row < 2 * factors) & (lax.rem(row, factors) == iota((width, factors), 1))
    for copy in copies[:2]:
        copy.wait()
    gate_all = gates_in[...]
    normed = gate_all / jnp.sum(gate_all, axis=0, keepdims=True)
    named = jnp.zeros((width, count), jnp.float32)
    gate = jnp.zeros((width, count), jnp.float32)
    for k in range(routes.shape[0]):
        hit = routes_in[k : k + 1, :] == expert
        named = jnp.where(hit, 1.0, named)
        gate = jnp.where(hit, normed[k : k + 1, :], gate)
    slot = jnp.dot(named.astype(jnp.bfloat16), after_it, preferred_element_type=jnp.float32)
    slot = jnp.where(named > 0.0, slot, -1.0)
    copies[2].wait()
    left = jnp.dot(
        pick.astype(jnp.bfloat16), table_in[...], preferred_element_type=jnp.float32
    ).astype(jnp.bfloat16)
    copies[3].wait()
    low_rank = lax.dot_general(left, rows_in[...], NT, preferred_element_type=jnp.float32)
    value = jnp.where(line < 3 * experts_all, gate, low_rank)
    high = value.astype(jnp.bfloat16).astype(jnp.float32)
    is_low = ((line >= 2 * experts_all) & (line < 3 * experts_all)) | (
        line >= 3 * experts_all + factors
    )
    value = jnp.where(is_low, value - high, high)
    info[...] = jnp.where(line < experts_all, slot, value).T.astype(jnp.bfloat16)
    for j, piece in enumerate(pieces):
        at = pl.multiple_of(lax.rem(my_part() - j + parts, parts) * rows, rows)
        piece[:, :model_width] = rows_in[pl.ds(at, rows), :]
        piece[:, model_width:] = info[pl.ds(at, rows), :]
    for copy in loads:
        copy.wait()


def up_kernel(first, load, experts_all, parts, cores, splits, capacity, factors, *refs):
    count = parts * (1 + (cores - 1) * splits)
    pieces = refs[:count]
    tiles_first, weight, right, seeds_in, *rest = refs[count:-5]
    down_weight = rest.pop(0) if load else None
    hidden, gate_out, *tiles_rest = rest
    down_tiles = tiles_rest.pop() if load else None
    block, slots, right_in, seeds, sems = refs[-5:]
    rows = pieces[0].shape[0]
    tok_count = rows * parts
    tiles_rest = tiles_rest[0] if first else weight
    local_experts, _, hid = hidden.shape
    steps, model_width, tile = tiles_first.shape
    width = block.shape[1] - model_width
    expert_rows = cores * capacity
    slot_count = local_experts * expert_rows

    tables = [
        pltpu.make_async_copy(right, right_in, sems.at[0]),
        pltpu.make_async_copy(seeds_in, seeds, sems.at[1]),
    ]
    copies = []
    if first:
        copies = [
            pltpu.make_async_copy(
                weight.at[l, :, pl.ds(n * tile, tile)],
                tiles_rest.at[(l - 1) * steps + n],
                sems.at[2 + (l - 1) * steps + n],
            )
            for l in range(1, local_experts)
            for n in range(steps)
        ]
    loads = []
    if load:
        down_steps = down_tiles.shape[0] // local_experts
        down_tile = down_tiles.shape[1]
        loads = [
            pltpu.make_async_copy(
                down_weight.at[l, pl.ds(n * down_tile, down_tile), :],
                down_tiles.at[l * down_steps + n],
                sems.at[2 + len(copies) + l * down_steps + n],
            )
            for l in range(local_experts)
            for n in range(down_steps)
        ]
    for copy in tables + copies + loads:
        copy.start()

    column = iota((width, 2 * slot_count), 0)
    slot = iota((width, 2 * slot_count), 1)
    owner = first_expert(local_experts) + lax.rem(slot, slot_count) // expert_rows
    place_of = (column == owner).astype(jnp.bfloat16)
    gate_of = (
        column == owner + jnp.where(slot < slot_count, experts_all, 2 * experts_all)
    ).astype(jnp.bfloat16)
    lane = iota((tok_count, 2 * slot_count), 1)
    wanted = lax.rem(lane, capacity).astype(jnp.float32)
    base = 0
    for piece in pieces:
        block[base : base + piece.shape[0], :] = piece[...]
        base += piece.shape[0]
    choosers = []
    for b in range(cores):
        base = b * tok_count
        info = block[base : base + tok_count, model_width:]
        slot_of = jnp.dot(info, place_of, preferred_element_type=jnp.float32)
        gate = jnp.dot(info, gate_of, preferred_element_type=jnp.float32)
        here = (slot_of == wanted) & (lax.rem(lane, expert_rows) // capacity == b)
        gate = jnp.where(here, gate, 0.0).astype(jnp.bfloat16)
        for j in range(parts):
            at = lax.rem(my_part() - j + parts, parts) * rows
            gate_out[pl.ds(pl.multiple_of(base + at, rows), rows), :] = gate[
                j * rows : (j + 1) * rows, :
            ]
        choosers.append(here[:, :slot_count].astype(jnp.bfloat16))
    slots[...] = lax.dot_general(
        jnp.concatenate(choosers, axis=0), block[...], TN, preferred_element_type=jnp.float32
    ).astype(jnp.bfloat16)

    for copy in tables:
        copy.wait()
    table = right_in[...].astype(jnp.float32)
    for l in range(local_experts):
        mine = slice(l * expert_rows, (l + 1) * expert_rows)
        extra = slots[mine, model_width:].astype(jnp.float32)
        at = iota(extra.shape, 1) - 3 * experts_all
        low_rank = jnp.sum(
            jnp.where((at == seeds[l, 0]) | (at == factors + seeds[l, 0]), extra, 0.0),
            axis=1,
            keepdims=True,
        )
        right_row = jnp.sum(
            jnp.where(iota(table.shape, 0) == seeds[l, 1], table, 0.0), axis=0, keepdims=True
        )
        for n in range(steps):
            if first and l > 0:
                copies[(l - 1) * steps + n].wait()
            tile_in = tiles_rest[(l - 1) * steps + n] if l > 0 else tiles_first[n]
            up_act = jnp.dot(
                slots[mine, :model_width], tile_in, preferred_element_type=jnp.float32
            )
            here = slice(n * tile, (n + 1) * tile)
            up_act = jnp.maximum(up_act + low_rank * right_row[:, here], 0.0)
            hidden[l, :, here] = (up_act * up_act).astype(jnp.bfloat16)
    for copy in loads:
        copy.wait()


def down_kernel(parts, cores, pieces_out, *refs):
    pieces = refs[:parts]
    tiles, left, right, seeds_in, gate, own, *rest = refs[parts:]
    others, (results, left_in, right_in, seeds, sems) = rest[:-5], rest[-5:]
    local_experts, expert_rows, depth = pieces[0].shape
    steps = tiles.shape[0] // local_experts
    tile = tiles.shape[1]
    slot_count = local_experts * expert_rows
    tok_count = gate.shape[0] // cores

    tables = [
        pltpu.make_async_copy(left, left_in, sems.at[0]),
        pltpu.make_async_copy(right, right_in, sems.at[1]),
        pltpu.make_async_copy(seeds_in, seeds, sems.at[2]),
    ]
    for copy in tables:
        copy.start()

    columns = [slice(None)]
    if parts > 1:
        columns = [
            pl.ds(pl.multiple_of(lax.rem(my_part() - j + parts, parts) * depth, depth), depth)
            for j in range(parts)
        ]
    for copy in tables:
        copy.wait()
    for l in range(local_experts):
        rank_all = sum(
            lax.dot_general(left_in[:, at], piece[l], NT, preferred_element_type=jnp.float32)
            for at, piece in zip(columns, pieces)
        )
        rank = jnp.sum(
            jnp.where(iota(rank_all.shape, 0) == seeds[l, 2], rank_all, 0.0),
            axis=0,
            keepdims=True,
        )
        chosen = (iota((right.shape[0], expert_rows), 0) == seeds[l, 3]).astype(jnp.bfloat16)
        for n in range(steps):
            result = sum(
                lax.dot_general(
                    tiles[l * steps + n, :, at], piece[l], NT, preferred_element_type=jnp.float32
                )
                for at, piece in zip(columns, pieces)
            )
            here = slice(n * tile, (n + 1) * tile)
            right_column = lax.dot_general(
                right_in[:, here], chosen, TN, preferred_element_type=jnp.float32
            )
            result = (result + right_column * rank).astype(jnp.bfloat16)
            for half in range(2):
                at = half * slot_count + l * expert_rows
                results[here, at : at + expert_rows] = result
    summed = lax.dot_general(results[...], gate[...], NT, preferred_element_type=jnp.float32)
    own[...] = summed[:, :tok_count]
    step = summed.shape[0] // pieces_out
    for b in range(1, cores):
        for i in range(pieces_out):
            others[(b - 1) * pieces_out + i][...] = summed[
                i * step : (i + 1) * step, b * tok_count : (b + 1) * tok_count
            ].astype(jnp.bfloat16)


def on_device(
    tokens,
    routes,
    route_gates,
    up_weight,
    down_weight,
    factor_seeds,
    up_left,
    up_right,
    down_left,
    down_right,
):
    chips, cores, parts = lax.axis_size("ctx"), lax.axis_size("tp"), lax.axis_size("exp")
    local_experts, model_width, hid = up_weight.shape
    hid_all, out_width = down_weight.shape[1:]
    experts_all = chips * cores * local_experts
    tok_count, top_count = routes.shape
    factors = up_left.shape[0]
    capacity = 4 * tok_count * top_count // (3 * experts_all)
    rows = tok_count // parts
    width = -(-(3 * experts_all + 2 * factors) // LANES) * LANES
    packed = model_width + width
    expert_rows = cores * capacity
    slot_count = local_experts * expert_rows
    all_tokens = cores * tok_count
    whole_tiles = hid % LANES == 0
    params = pltpu.CompilerParams(vmem_limit_bytes=VMEM_LIMIT)
    vmem, hbm = (pl.BlockSpec(memory_space=space) for space in (pltpu.VMEM, pltpu.HBM))
    up_steps = 3 if hid % (3 * LANES) == 0 else 1
    up_tiles = (up_steps, model_width, hid // up_steps)

    prep = pl.pallas_call(
        functools.partial(prep_kernel, experts_all, parts),
        out_shape=[jax.ShapeDtypeStruct((rows, packed), jnp.bfloat16)] * parts
        + [jax.ShapeDtypeStruct(up_tiles, jnp.bfloat16)],
        in_specs=[hbm] * 5,
        out_specs=[vmem] * (parts + 1),
        scratch_shapes=[
            pltpu.VMEM((top_count, tok_count), jnp.int32),
            pltpu.VMEM((top_count, tok_count), jnp.float32),
            pltpu.VMEM(tokens.shape, jnp.bfloat16),
            pltpu.VMEM(up_left.shape, jnp.bfloat16),
            pltpu.VMEM((tok_count, width), jnp.bfloat16),
            pltpu.SemaphoreType.DMA((4 + up_steps,)),
        ],
        compiler_params=params,
        name="pack_tokens",
    )

    splits = 2 if rows % 32 == 0 else 1
    up_rest = ((local_experts - 1) * up_steps,) + up_tiles[1:]

    down_steps = 3 if out_width % 48 == 0 else 1
    down_tiles = (local_experts * down_steps, out_width // down_steps, hid_all)

    def up(first, load):
        return pl.pallas_call(
            functools.partial(
                up_kernel, first, load, experts_all, parts, cores, splits, capacity, factors
            ),
            out_shape=[
                jax.ShapeDtypeStruct((local_experts, expert_rows, hid), jnp.bfloat16),
                jax.ShapeDtypeStruct((all_tokens, 2 * slot_count), jnp.bfloat16),
            ]
            + [jax.ShapeDtypeStruct(up_rest, jnp.bfloat16)] * first
            + [jax.ShapeDtypeStruct(down_tiles, jnp.bfloat16)] * load,
            in_specs=[vmem] * (parts * (1 + (cores - 1) * splits))
            + [vmem, hbm if first else vmem, hbm, hbm]
            + [hbm] * load,
            out_specs=[vmem] * (2 + first + load),
            scratch_shapes=[
                pltpu.VMEM((all_tokens, packed), jnp.bfloat16),
                pltpu.VMEM((slot_count, packed), jnp.bfloat16),
                pltpu.VMEM(up_right.shape, jnp.bfloat16),
                pltpu.SMEM(factor_seeds.shape, jnp.int32),
                pltpu.SemaphoreType.DMA((2 + (local_experts - 1) * up_steps + down_tiles[0],)),
            ],
            compiler_params=params,
            name="up",
        )

    r_splits = 2 if out_width % 64 == 0 else 1
    hidden_parts = parts if whole_tiles else 1

    down = pl.pallas_call(
        functools.partial(down_kernel, hidden_parts, cores, r_splits),
        out_shape=[jax.ShapeDtypeStruct((out_width, tok_count), jnp.float32)]
        + [jax.ShapeDtypeStruct((out_width // r_splits, tok_count), jnp.bfloat16)]
        * ((cores - 1) * r_splits),
        in_specs=[vmem] * (hidden_parts + 1) + [hbm, hbm, hbm, vmem],
        out_specs=[vmem] * (1 + (cores - 1) * r_splits),
        scratch_shapes=[
            pltpu.VMEM((out_width, 2 * slot_count), jnp.bfloat16),
            pltpu.VMEM(down_left.shape, jnp.bfloat16),
            pltpu.VMEM(down_right.shape, jnp.bfloat16),
            pltpu.SMEM(factor_seeds.shape, jnp.int32),
            pltpu.SemaphoreType.DMA((3,)),
        ],
        compiler_params=params,
        name="down",
    )

    in_hbm = [
        in_memory(value, pltpu.HBM)
        for value in (
            routes.T, route_gates.T, tokens, up_left, up_weight, up_right,
            down_weight.transpose(0, 2, 1), down_left, down_right, factor_seeds,
        )
    ]
    up_weight, up_right, down_turned, down_left, down_right, seeds = in_hbm[4:]
    *pieces, tiles_first = prep(*in_hbm[:5])
    kept = {}

    last = [pieces[0]]

    def order(value):
        last[0] = after(value, last[0])
        return last[0]

    def over_cores(piece):
        step = rows // splits
        return [
            [shift(piece[i * step : (i + 1) * step], "tp", b) for i in range(splits)]
            for b in range(1, cores)
        ]

    def over_exp(value):
        return [shift(value, "exp", j) for j in range(1, parts)]

    def up_only(here, there, load=False):
        blocks = here + [
            there[j][b][i] for b in range(cores - 1) for j in range(parts) for i in range(splits)
        ]
        first = "up" not in kept
        hidden, gate, *tiles = up(first, load)(
            order(blocks[0]),
            *blocks[1:],
            tiles_first,
            up_weight if first else kept["up"],
            up_right,
            seeds,
            *([down_turned] if load else []),
        )
        if load:
            kept["down"] = tiles.pop()
        if first:
            kept["up"] = tiles[0]
        last[0] = gate
        return hidden, gate

    def exchanged(hidden):
        if whole_tiles:
            return [hidden] + over_exp(hidden)
        return [lax.all_gather(hidden, "exp", axis=2, tiled=True)]

    def run_down(hiddens, gate):
        own, *others = down(
            *hiddens[:-1],
            order(hiddens[-1]),
            kept["down"],
            down_left,
            down_right,
            seeds,
            gate,
        )
        last[0] = own
        return own, others

    def back(others):
        return [
            [shift(others[(b - 1) * r_splits + i], "tp", -b) for i in range(r_splits)]
            for b in range(1, cores)
        ]

    def add(own, swapped, *values):
        arrays = [piece for pieces in swapped for piece in pieces]

        def kernel(own, *refs):
            out, refs = refs[-1], refs[:-1]
            step = own.shape[0] // r_splits
            for i in range(r_splits):
                at = slice(i * step, (i + 1) * step)
                total = own[at, :]
                for b in range(cores - 1):
                    total = total + refs[b * r_splits + i][...].astype(jnp.float32)
                for value in refs[len(arrays) :]:
                    total = total + value[at, :].astype(jnp.float32)
                out[at, :] = total.astype(jnp.bfloat16)

        return pl.pallas_call(
            kernel,
            out_shape=jax.ShapeDtypeStruct(own.shape, jnp.bfloat16),
            in_specs=[vmem] * (1 + len(arrays) + len(values)),
            out_specs=vmem,
            compiler_params=params,
            cost_estimate=pl.CostEstimate(flops=1, bytes_accessed=1, transcendentals=0),
            name="add",
        )(own, *arrays, *values)

    def summed(own, others, *more):
        return add(own, back(others), *more)

    returned = {}

    def give_back(k, own, others):
        total = order(
            summed(own, [after(others[0], last[0])] + others[1:], *([returned[k - 1]] if k > 2 else []))
        )
        returned[k] = shift(total, "ctx", -1 if k == 1 else 1)

    def send_direct(earlier):
        return [shift(after(piece, earlier), "ctx", -1) for piece in pieces[1:]]

    arriving = shift(pieces[0], "ctx", 1)
    direct = [shift(piece, "ctx", -1) for piece in pieces[1:]]
    hidden_own, gate_own = up_only(pieces, [over_cores(piece) for piece in pieces], load=True)
    arriving = order(arriving)
    direct = [order(piece) for piece in direct]
    mine_there = over_cores(arriving)
    work = [None]
    for k in range(1, chips):
        here = [arriving] + (over_exp(arriving) if k < chips - 1 else direct)
        there = [mine_there]
        if k < chips - 1:
            arriving = shift(arriving, "ctx", 1)
        if k == 1:
            arriving = order(arriving)
        here[1:] = [order(piece) for piece in here[1:]]
        there += [over_cores(piece) for piece in here[1:]]
        if k < chips - 2:
            mine_there = over_cores(arriving)
            mine_there = [[order(half) for half in halves] for halves in mine_there]
        hidden, gate = up_only(here, there)
        work.append((exchanged(hidden), gate))
        if 1 < k < chips - 1:
            arriving = order(arriving)
            if k == chips - 2:
                mine_there = over_cores(arriving)
    hidden_own = after(hidden_own, gate)
    work[0] = (exchanged(hidden_own), gate_own)
    for k in range(1, chips):
        sums = run_down(*work[k])
        give_back(k, *sums)
        if 1 < k == chips - 2:
            returned[1] = order(returned[1])
    own_sum, own_others = run_down(*work[0])
    homeward = {1, chips - 1}
    return add(own_sum, back(own_others), *(returned[k] for k in sorted(homeward))).T


def solution(mesh):
    in_specs = (
        P(("pop", "ctx", "tp"), None),
        P(("pop", "ctx", "tp"), None),
        P(("pop", "ctx", "tp"), None),
        P(("ctx", "tp"), None, "exp"),
        P(("ctx", "tp"), None, "exp"),
        P(("pop", "ctx", "tp"), None),
        P(),
        P(None, "exp"),
        P(),
        P(None, "exp"),
    )
    out_specs = P(("pop", "ctx", "tp"), "exp")
    return jax.shard_map(
        on_device, mesh=mesh, in_specs=in_specs, out_specs=out_specs, check_vma=False
    )
```

```python
import functools

import jax
import jax.numpy as jnp
from jax import lax
from jax.experimental import pallas as pl
from jax.experimental.pallas import tpu as pltpu
from jax.sharding import PartitionSpec as P

LANES = 128
VMEM_LIMIT = 24 * 1024 * 1024
NT = (((1,), (1,)), ((), ()))
TN = (((0,), (0,)), ((), ()))


def shift(value, axis, by):
    size = lax.axis_size(axis)
    return lax.ppermute(value, axis, [(i, (i + by) % size) for i in range(size)])


in_memory = pltpu.with_memory_space_constraint


def after(value, earlier):
    return lax.optimization_barrier((value, earlier))[0]


def iota(shape, dim):
    return lax.broadcasted_iota(jnp.int32, shape, dim)


def my_part():
    return lax.axis_index("exp")


def first_expert(local_experts):
    return (lax.axis_index("ctx") * lax.axis_size("tp") + lax.axis_index("tp")) * local_experts


def prep_kernel(experts_all, parts, routes, gates, tokens, up_left, weight, *refs):
    pieces, tiles = refs[:parts], refs[parts]
    routes_in, gates_in, rows_in, table_in, info, sems = refs[parts + 1 :]
    count, model_width = tokens.shape
    width = info.shape[1]
    factors = up_left.shape[0]
    rows = count // parts
    copies = [
        pltpu.make_async_copy(source, target, sems.at[i])
        for i, (source, target) in enumerate(
            ((routes, routes_in), (gates, gates_in), (up_left, table_in), (tokens, rows_in))
        )
    ]
    steps, _, tile = tiles.shape
    loads = [
        pltpu.make_async_copy(
            weight.at[0, :, pl.ds(n * tile, tile)], tiles.at[n], sems.at[len(copies) + n]
        )
        for n in range(steps)
    ]
    for copy in copies + loads:
        copy.start()
    line = iota((width, count), 0)
    expert = lax.rem(line, experts_all)
    after_it = (iota((count, count), 0) < iota((count, count), 1)).astype(jnp.bfloat16)
    row = iota((width, factors), 0) - 2 * experts_all
    pick = (row >= 0) & (row < 2 * factors) & (lax.rem(row, factors) == iota((width, factors), 1))
    for copy in copies[:2]:
        copy.wait()
    gate_all = gates_in[...]
    normed = gate_all / jnp.sum(gate_all, axis=0, keepdims=True)
    named = jnp.zeros((width, count), jnp.float32)
    gate = jnp.zeros((width, count), jnp.float32)
    for k in range(routes.shape[0]):
        hit = routes_in[k : k + 1, :] == expert
        named = jnp.where(hit, 1.0, named)
        gate = jnp.where(hit, normed[k : k + 1, :], gate)
    slot = jnp.dot(named.astype(jnp.bfloat16), after_it, preferred_element_type=jnp.float32)
    slot = jnp.where(named > 0.0, slot, -1.0)
    copies[2].wait()
    left = jnp.dot(
        pick.astype(jnp.bfloat16), table_in[...], preferred_element_type=jnp.float32
    ).astype(jnp.bfloat16)
    copies[3].wait()
    low_rank = lax.dot_general(left, rows_in[...], NT, preferred_element_type=jnp.float32)
    value = jnp.where(line < 2 * experts_all, gate, low_rank)
    high = value.astype(jnp.bfloat16).astype(jnp.float32)
    is_low = line >= 2 * experts_all + factors
    value = jnp.where(is_low, value - high, high)
    info[...] = jnp.where(line < experts_all, slot, value).T.astype(jnp.bfloat16)
    for j, piece in enumerate(pieces):
        at = pl.multiple_of(lax.rem(my_part() - j + parts, parts) * rows, rows)
        piece[:, :model_width] = rows_in[pl.ds(at, rows), :]
        piece[:, model_width:] = info[pl.ds(at, rows), :]
    for copy in loads:
        copy.wait()


def up_kernel(first, load, count, rows, experts_all, parts, cores, capacity, factors, *refs):
    pieces = refs[:count]
    tiles_first, weight, right, seeds_in, *rest = refs[count:-5]
    down_weight = rest.pop(0) if load else None
    hidden, gate_out, *tiles_rest = rest
    down_tiles = tiles_rest.pop() if load else None
    block, slots, right_in, seeds, sems = refs[-5:]
    tok_count = rows * parts
    tiles_rest = tiles_rest[0] if first else weight
    local_experts, _, hid = hidden.shape
    steps, model_width, tile = tiles_first.shape
    width = block.shape[1] - model_width
    expert_rows = cores * capacity
    slot_count = local_experts * expert_rows

    tables = [
        pltpu.make_async_copy(right, right_in, sems.at[0]),
        pltpu.make_async_copy(seeds_in, seeds, sems.at[1]),
    ]
    copies = []
    if first:
        copies = [
            pltpu.make_async_copy(
                weight.at[l, :, pl.ds(n * tile, tile)],
                tiles_rest.at[(l - 1) * steps + n],
                sems.at[2 + (l - 1) * steps + n],
            )
            for l in range(1, local_experts)
            for n in range(steps)
        ]
    loads = []
    if load:
        down_steps = down_tiles.shape[0] // local_experts
        down_tile = down_tiles.shape[1]
        loads = [
            pltpu.make_async_copy(
                down_weight.at[l, pl.ds(n * down_tile, down_tile), :],
                down_tiles.at[l * down_steps + n],
                sems.at[2 + len(copies) + l * down_steps + n],
            )
            for l in range(local_experts)
            for n in range(down_steps)
        ]
    for copy in tables + copies + loads:
        copy.start()

    column = iota((width, slot_count), 0)
    slot = iota((width, slot_count), 1)
    owner = first_expert(local_experts) + slot // expert_rows
    place_of = (column == owner).astype(jnp.bfloat16)
    gate_of = (column == owner + experts_all).astype(jnp.bfloat16)
    lane = iota((tok_count, slot_count), 1)
    wanted = lax.rem(lane, capacity).astype(jnp.float32)
    base = 0
    for piece in pieces:
        block[base : base + piece.shape[0], :] = piece[...]
        base += piece.shape[0]
    choosers = []
    for b in range(cores):
        base = b * tok_count
        info = block[base : base + tok_count, model_width:]
        slot_of = jnp.dot(info, place_of, preferred_element_type=jnp.float32)
        gate = jnp.dot(info, gate_of, preferred_element_type=jnp.float32)
        here = (slot_of == wanted) & (lax.rem(lane, expert_rows) // capacity == b)
        gate = jnp.where(here, gate, 0.0).astype(jnp.bfloat16)
        for j in range(parts):
            at = lax.rem(my_part() - j + parts, parts) * rows
            gate_out[pl.ds(pl.multiple_of(base + at, rows), rows), :] = gate[
                j * rows : (j + 1) * rows, :
            ]
        choosers.append(here.astype(jnp.bfloat16))
    slots[...] = lax.dot_general(
        jnp.concatenate(choosers, axis=0), block[...], TN, preferred_element_type=jnp.float32
    ).astype(jnp.bfloat16)

    for copy in tables:
        copy.wait()
    table = right_in[...].astype(jnp.float32)
    for l in range(local_experts):
        mine = slice(l * expert_rows, (l + 1) * expert_rows)
        extra = slots[mine, model_width:].astype(jnp.float32)
        at = iota(extra.shape, 1) - 2 * experts_all
        low_rank = jnp.sum(
            jnp.where((at == seeds[l, 0]) | (at == factors + seeds[l, 0]), extra, 0.0),
            axis=1,
            keepdims=True,
        )
        right_row = jnp.sum(
            jnp.where(iota(table.shape, 0) == seeds[l, 1], table, 0.0), axis=0, keepdims=True
        )
        for n in range(steps):
            if first and l > 0:
                copies[(l - 1) * steps + n].wait()
            tile_in = tiles_rest[(l - 1) * steps + n] if l > 0 else tiles_first[n]
            up_act = jnp.dot(
                slots[mine, :model_width], tile_in, preferred_element_type=jnp.float32
            )
            here = slice(n * tile, (n + 1) * tile)
            up_act = jnp.maximum(up_act + low_rank * right_row[:, here], 0.0)
            hidden[l, :, here] = (up_act * up_act).astype(jnp.bfloat16)
    for copy in loads:
        copy.wait()


def down_kernel(parts, cores, pieces_out, *refs):
    pieces = refs[:parts]
    tiles, left, right, seeds_in, gate, own, *rest = refs[parts:]
    others, (results, left_in, right_in, seeds, sems) = rest[:-5], rest[-5:]
    local_experts, expert_rows, depth = pieces[0].shape
    steps = tiles.shape[0] // local_experts
    tile = tiles.shape[1]
    slot_count = local_experts * expert_rows
    tok_count = gate.shape[0] // cores

    tables = [
        pltpu.make_async_copy(left, left_in, sems.at[0]),
        pltpu.make_async_copy(right, right_in, sems.at[1]),
        pltpu.make_async_copy(seeds_in, seeds, sems.at[2]),
    ]
    for copy in tables:
        copy.start()

    columns = [slice(None)]
    if parts > 1:
        columns = [
            pl.ds(pl.multiple_of(lax.rem(my_part() - j + parts, parts) * depth, depth), depth)
            for j in range(parts)
        ]
    for copy in tables:
        copy.wait()
    for l in range(local_experts):
        rank_all = sum(
            lax.dot_general(left_in[:, at], piece[l], NT, preferred_element_type=jnp.float32)
            for at, piece in zip(columns, pieces)
        )
        rank = jnp.sum(
            jnp.where(iota(rank_all.shape, 0) == seeds[l, 2], rank_all, 0.0),
            axis=0,
            keepdims=True,
        )
        chosen = (iota((right.shape[0], expert_rows), 0) == seeds[l, 3]).astype(jnp.bfloat16)
        for n in range(steps):
            result = sum(
                lax.dot_general(
                    tiles[l * steps + n, :, at], piece[l], NT, preferred_element_type=jnp.float32
                )
                for at, piece in zip(columns, pieces)
            )
            here = slice(n * tile, (n + 1) * tile)
            right_column = lax.dot_general(
                right_in[:, here], chosen, TN, preferred_element_type=jnp.float32
            )
            result = (result + right_column * rank).astype(jnp.bfloat16)
            results[here, l * expert_rows : (l + 1) * expert_rows] = result
    summed = lax.dot_general(results[...], gate[...], NT, preferred_element_type=jnp.float32)
    own[...] = summed[:, :tok_count]
    step = summed.shape[0] // pieces_out
    for b in range(1, cores):
        for i in range(pieces_out):
            others[(b - 1) * pieces_out + i][...] = summed[
                i * step : (i + 1) * step, b * tok_count : (b + 1) * tok_count
            ].astype(jnp.bfloat16)


def on_device(
    tokens,
    routes,
    route_gates,
    up_weight,
    down_weight,
    factor_seeds,
    up_left,
    up_right,
    down_left,
    down_right,
):
    chips, cores, parts = lax.axis_size("ctx"), lax.axis_size("tp"), lax.axis_size("exp")
    local_experts, model_width, hid = up_weight.shape
    hid_all, out_width = down_weight.shape[1:]
    experts_all = chips * cores * local_experts
    tok_count, top_count = routes.shape
    factors = up_left.shape[0]
    capacity = 4 * tok_count * top_count // (3 * experts_all)
    rows = tok_count // parts
    width = -(-2 * (experts_all + factors) // LANES) * LANES
    packed = model_width + width
    expert_rows = cores * capacity
    slot_count = local_experts * expert_rows
    all_tokens = cores * tok_count
    whole_tiles = hid % LANES == 0
    params = pltpu.CompilerParams(vmem_limit_bytes=VMEM_LIMIT)
    vmem, hbm = (pl.BlockSpec(memory_space=space) for space in (pltpu.VMEM, pltpu.HBM))
    up_steps = 3 if hid % (3 * LANES) == 0 else 1
    up_tiles = (up_steps, model_width, hid // up_steps)

    prep = pl.pallas_call(
        functools.partial(prep_kernel, experts_all, parts),
        out_shape=[jax.ShapeDtypeStruct((rows, packed), jnp.bfloat16)] * parts
        + [jax.ShapeDtypeStruct(up_tiles, jnp.bfloat16)],
        in_specs=[hbm] * 5,
        out_specs=[vmem] * (parts + 1),
        scratch_shapes=[
            pltpu.VMEM((top_count, tok_count), jnp.int32),
            pltpu.VMEM((top_count, tok_count), jnp.float32),
            pltpu.VMEM(tokens.shape, jnp.bfloat16),
            pltpu.VMEM(up_left.shape, jnp.bfloat16),
            pltpu.VMEM((tok_count, width), jnp.bfloat16),
            pltpu.SemaphoreType.DMA((4 + up_steps,)),
        ],
        compiler_params=params,
        name="pack_tokens",
    )

    splits = 2 if rows % 32 == 0 else 1
    up_rest = ((local_experts - 1) * up_steps,) + up_tiles[1:]

    down_steps = 3 if out_width % 48 == 0 else 1
    down_tiles = (local_experts * down_steps, out_width // down_steps, hid_all)

    def up(first, load, count):
        return pl.pallas_call(
            functools.partial(
                up_kernel, first, load, count, rows, experts_all, parts, cores, capacity, factors
            ),
            out_shape=[
                jax.ShapeDtypeStruct((local_experts, expert_rows, hid), jnp.bfloat16),
                jax.ShapeDtypeStruct((all_tokens, slot_count), jnp.bfloat16),
            ]
            + [jax.ShapeDtypeStruct(up_rest, jnp.bfloat16)] * first
            + [jax.ShapeDtypeStruct(down_tiles, jnp.bfloat16)] * load,
            in_specs=[vmem] * count
            + [vmem, hbm if first else vmem, hbm, hbm]
            + [hbm] * load,
            out_specs=[vmem] * (2 + first + load),
            scratch_shapes=[
                pltpu.VMEM((all_tokens, packed), jnp.bfloat16),
                pltpu.VMEM((slot_count, packed), jnp.bfloat16),
                pltpu.VMEM(up_right.shape, jnp.bfloat16),
                pltpu.SMEM(factor_seeds.shape, jnp.int32),
                pltpu.SemaphoreType.DMA((2 + (local_experts - 1) * up_steps + down_tiles[0],)),
            ],
            compiler_params=params,
            name="up",
        )

    r_splits = 2 if out_width % 64 == 0 else 1
    hidden_parts = parts if whole_tiles else 1

    down = pl.pallas_call(
        functools.partial(down_kernel, hidden_parts, cores, r_splits),
        out_shape=[jax.ShapeDtypeStruct((out_width, tok_count), jnp.float32)]
        + [jax.ShapeDtypeStruct((out_width // r_splits, tok_count), jnp.bfloat16)]
        * ((cores - 1) * r_splits),
        in_specs=[vmem] * (hidden_parts + 1) + [hbm, hbm, hbm, vmem],
        out_specs=[vmem] * (1 + (cores - 1) * r_splits),
        scratch_shapes=[
            pltpu.VMEM((out_width, slot_count), jnp.bfloat16),
            pltpu.VMEM(down_left.shape, jnp.bfloat16),
            pltpu.VMEM(down_right.shape, jnp.bfloat16),
            pltpu.SMEM(factor_seeds.shape, jnp.int32),
            pltpu.SemaphoreType.DMA((3,)),
        ],
        compiler_params=params,
        name="down",
    )

    in_hbm = [
        in_memory(value, pltpu.HBM)
        for value in (
            routes.T, route_gates.T, tokens, up_left, up_weight, up_right,
            down_weight.transpose(0, 2, 1), down_left, down_right, factor_seeds,
        )
    ]
    up_weight, up_right, down_turned, down_left, down_right, seeds = in_hbm[4:]
    *pieces, tiles_first = prep(*in_hbm[:5])
    kept = {}

    last = [pieces[0]]

    def order(value):
        last[0] = after(value, last[0])
        return last[0]

    def halves_of(piece):
        step = rows // splits
        return [piece[i * step : (i + 1) * step] for i in range(splits)]

    def over_cores(halves):
        return [[shift(half, "tp", b) for half in halves] for b in range(1, cores)]

    def over_exp(value):
        return [shift(value, "exp", j) for j in range(1, parts)]

    def up_only(here, there, load=False):
        blocks = [half for halves in here for half in halves]
        for b in range(cores - 1):
            blocks += [half for others in there for half in others[b]]
        first = "up" not in kept
        hidden, gate, *tiles = up(first, load, len(blocks))(
            order(blocks[0]),
            *blocks[1:],
            tiles_first,
            up_weight if first else kept["up"],
            up_right,
            seeds,
            *([down_turned] if load else []),
        )
        if load:
            kept["down"] = tiles.pop()
        if first:
            kept["up"] = tiles[0]
        last[0] = gate
        return hidden, gate

    def exchanged(hidden):
        if whole_tiles:
            return [hidden] + over_exp(hidden)
        return [lax.all_gather(hidden, "exp", axis=2, tiled=True)]

    def run_down(hiddens, gate):
        own, *others = down(
            *hiddens[:-1],
            order(hiddens[-1]),
            kept["down"],
            down_left,
            down_right,
            seeds,
            gate,
        )
        last[0] = own
        return own, others

    def back(others):
        return [
            [shift(others[(b - 1) * r_splits + i], "tp", -b) for i in range(r_splits)]
            for b in range(1, cores)
        ]

    def add(own, swapped, *values):
        arrays = [piece for pieces in swapped for piece in pieces]

        def kernel(own, *refs):
            out, refs = refs[-1], refs[:-1]
            step = own.shape[0] // r_splits
            for i in range(r_splits):
                at = slice(i * step, (i + 1) * step)
                total = own[at, :]
                for b in range(cores - 1):
                    total = total + refs[b * r_splits + i][...].astype(jnp.float32)
                for value in refs[len(arrays) :]:
                    total = total + value[at, :].astype(jnp.float32)
                out[at, :] = total.astype(jnp.bfloat16)

        return pl.pallas_call(
            kernel,
            out_shape=jax.ShapeDtypeStruct(own.shape, jnp.bfloat16),
            in_specs=[vmem] * (1 + len(arrays) + len(values)),
            out_specs=vmem,
            compiler_params=params,
            cost_estimate=pl.CostEstimate(flops=1, bytes_accessed=1, transcendentals=0),
            name="add",
        )(own, *arrays, *values)

    def summed(own, others, *more):
        return add(own, back(others), *more)

    returned = {}

    def give_back(k, own, others):
        total = order(
            summed(own, [after(others[0], last[0])] + others[1:], *([returned[k - 1]] if k > 2 else []))
        )
        returned[k] = shift(total, "ctx", -1 if k == 1 else 1)

    def send_direct(earlier):
        return [shift(after(piece, earlier), "ctx", -1) for piece in pieces[1:]]

    arriving = shift(pieces[0], "ctx", 1)
    direct = [halves_of(piece) for piece in pieces[1:]]
    direct = [[shift(halves[0], "ctx", -1)] + halves[1:] for halves in direct]
    hidden_own, gate_own = up_only(
        [[piece] for piece in pieces],
        [over_cores(halves_of(piece)) for piece in pieces],
        load=True,
    )
    arriving = order(arriving)
    direct = [[order(halves[0])] + halves[1:] for halves in direct]
    mine_there = over_cores(halves_of(arriving))
    work = [None]
    for k in range(1, chips):
        if k == max(1, chips - 2):
            direct = [
                halves[:1] + [shift(after(half, arriving), "ctx", -1) for half in halves[1:]]
                for halves in direct
            ]
        if k < chips - 1:
            here = [[piece] for piece in [arriving] + over_exp(arriving)]
        else:
            here = [[arriving]] + direct
        there = [mine_there]
        if k < chips - 1:
            arriving = shift(arriving, "ctx", 1)
        if k == 1:
            arriving = order(arriving)
        here[1:] = [halves[:-1] + [order(halves[-1])] for halves in here[1:]]
        there += [
            over_cores(halves_of(halves[0]) if len(halves) == 1 else halves) for halves in here[1:]
        ]
        if k < chips - 2:
            mine_there = over_cores(halves_of(arriving))
        hidden, gate = up_only(here, there)
        work.append((exchanged(hidden), gate))
        if 1 < k < chips - 1:
            arriving = order(arriving)
            if k == chips - 2:
                mine_there = over_cores(halves_of(arriving))
    hidden_own = after(hidden_own, gate)
    work[0] = (exchanged(hidden_own), gate_own)
    for k in range(1, chips):
        sums = run_down(*work[k])
        give_back(k, *sums)
        if 1 < k == chips - 2:
            returned[1] = order(returned[1])
    own_sum, own_others = run_down(*work[0])
    homeward = {1, chips - 1}
    return add(own_sum, back(own_others), *(returned[k] for k in sorted(homeward))).T


def solution(mesh):
    in_specs = (
        P(("pop", "ctx", "tp"), None),
        P(("pop", "ctx", "tp"), None),
        P(("pop", "ctx", "tp"), None),
        P(("ctx", "tp"), None, "exp"),
        P(("ctx", "tp"), None, "exp"),
        P(("pop", "ctx", "tp"), None),
        P(),
        P(None, "exp"),
        P(),
        P(None, "exp"),
    )
    out_specs = P(("pop", "ctx", "tp"), "exp")
    return jax.shard_map(
        on_device, mesh=mesh, in_specs=in_specs, out_specs=out_specs, check_vma=False
    )
```

```python
import functools

import jax
import jax.numpy as jnp
from jax import lax
from jax.experimental import pallas as pl
from jax.experimental.pallas import tpu as pltpu
from jax.sharding import PartitionSpec as P

LANES = 128
VMEM_LIMIT = 24 * 1024 * 1024
NT = (((1,), (1,)), ((), ()))
TN = (((0,), (0,)), ((), ()))


def shift(value, axis, by):
    size = lax.axis_size(axis)
    return lax.ppermute(value, axis, [(i, (i + by) % size) for i in range(size)])


in_memory = pltpu.with_memory_space_constraint


def after(value, earlier):
    return lax.optimization_barrier((value, earlier))[0]


def iota(shape, dim):
    return lax.broadcasted_iota(jnp.int32, shape, dim)


def my_part():
    return lax.axis_index("exp")


def first_expert(local_experts):
    return (lax.axis_index("ctx") * lax.axis_size("tp") + lax.axis_index("tp")) * local_experts


def prep_kernel(experts_all, parts, routes, gates, tokens, up_left, *refs):
    pieces, (routes_in, gates_in, rows_in, table_in, info, sems) = refs[:parts], refs[parts:]
    count, model_width = tokens.shape
    width = info.shape[1]
    factors = up_left.shape[0]
    rows = count // parts
    copies = [
        pltpu.make_async_copy(source, target, sems.at[i])
        for i, (source, target) in enumerate(
            ((routes, routes_in), (gates, gates_in), (up_left, table_in), (tokens, rows_in))
        )
    ]
    for copy in copies:
        copy.start()
    line = iota((width, count), 0)
    expert = lax.rem(line, experts_all)
    after_it = (iota((count, count), 0) < iota((count, count), 1)).astype(jnp.bfloat16)
    row = iota((width, factors), 0) - 2 * experts_all
    pick = (row >= 0) & (row < 2 * factors) & (lax.rem(row, factors) == iota((width, factors), 1))
    for copy in copies[:2]:
        copy.wait()
    gate_all = gates_in[...]
    normed = gate_all / jnp.sum(gate_all, axis=0, keepdims=True)
    named = jnp.zeros((width, count), jnp.float32)
    gate = jnp.zeros((width, count), jnp.float32)
    for k in range(routes.shape[0]):
        hit = routes_in[k : k + 1, :] == expert
        named = jnp.where(hit, 1.0, named)
        gate = jnp.where(hit, normed[k : k + 1, :], gate)
    slot = jnp.dot(named.astype(jnp.bfloat16), after_it, preferred_element_type=jnp.float32)
    slot = jnp.where(named > 0.0, slot, -1.0)
    copies[2].wait()
    left = jnp.dot(
        pick.astype(jnp.bfloat16), table_in[...], preferred_element_type=jnp.float32
    ).astype(jnp.bfloat16)
    copies[3].wait()
    low_rank = lax.dot_general(left, rows_in[...], NT, preferred_element_type=jnp.float32)
    value = jnp.where(line < 2 * experts_all, gate, low_rank)
    high = value.astype(jnp.bfloat16).astype(jnp.float32)
    is_low = line >= 2 * experts_all + factors
    value = jnp.where(is_low, value - high, high)
    info[...] = jnp.where(line < experts_all, slot, value).T.astype(jnp.bfloat16)
    for j, piece in enumerate(pieces):
        at = pl.multiple_of(lax.rem(my_part() - j + parts, parts) * rows, rows)
        piece[:, :model_width] = rows_in[pl.ds(at, rows), :]
        piece[:, model_width:] = info[pl.ds(at, rows), :]


def up_kernel(first, load, count, rows, experts_all, parts, cores, capacity, factors, *refs):
    pieces = refs[:count]
    weight, right, seeds_in, *rest = refs[count:-5]
    down_weight = rest.pop(0) if load else None
    hidden, gate_out, *tiles = rest
    down_tiles = tiles.pop() if load else None
    block, slots, right_in, seeds, sems = refs[-5:]
    tok_count = rows * parts
    tiles = tiles[0] if first else weight
    local_experts, _, hid = hidden.shape
    steps = tiles.shape[0] // local_experts
    model_width, tile = tiles.shape[1:]
    width = block.shape[1] - model_width
    expert_rows = cores * capacity
    slot_count = local_experts * expert_rows

    tables = [
        pltpu.make_async_copy(right, right_in, sems.at[0]),
        pltpu.make_async_copy(seeds_in, seeds, sems.at[1]),
    ]
    copies = []
    if first:
        copies = [
            pltpu.make_async_copy(
                weight.at[l, :, pl.ds(n * tile, tile)],
                tiles.at[l * steps + n],
                sems.at[2 + l * steps + n],
            )
            for l in range(local_experts)
            for n in range(steps)
        ]
    loads = []
    if load:
        down_steps = down_tiles.shape[0] // local_experts
        down_tile = down_tiles.shape[1]
        loads = [
            pltpu.make_async_copy(
                down_weight.at[l, pl.ds(n * down_tile, down_tile), :],
                down_tiles.at[l * down_steps + n],
                sems.at[2 + len(copies) + l * down_steps + n],
            )
            for l in range(local_experts)
            for n in range(down_steps)
        ]
    for copy in tables + copies + loads:
        copy.start()

    column = iota((width, slot_count), 0)
    slot = iota((width, slot_count), 1)
    owner = first_expert(local_experts) + slot // expert_rows
    place_of = (column == owner).astype(jnp.bfloat16)
    gate_of = (column == owner + experts_all).astype(jnp.bfloat16)
    lane = iota((tok_count, slot_count), 1)
    wanted = lax.rem(lane, capacity).astype(jnp.float32)
    base = 0
    for piece in pieces:
        block[base : base + piece.shape[0], :] = piece[...]
        base += piece.shape[0]
    choosers = []
    for b in range(cores):
        base = b * tok_count
        info = block[base : base + tok_count, model_width:]
        slot_of = jnp.dot(info, place_of, preferred_element_type=jnp.float32)
        gate = jnp.dot(info, gate_of, preferred_element_type=jnp.float32)
        here = (slot_of == wanted) & (lax.rem(lane, expert_rows) // capacity == b)
        gate = jnp.where(here, gate, 0.0).astype(jnp.bfloat16)
        for j in range(parts):
            at = lax.rem(my_part() - j + parts, parts) * rows
            gate_out[pl.ds(pl.multiple_of(base + at, rows), rows), :] = gate[
                j * rows : (j + 1) * rows, :
            ]
        choosers.append(here.astype(jnp.bfloat16))
    slots[...] = lax.dot_general(
        jnp.concatenate(choosers, axis=0), block[...], TN, preferred_element_type=jnp.float32
    ).astype(jnp.bfloat16)

    for copy in tables:
        copy.wait()
    table = right_in[...].astype(jnp.float32)
    for l in range(local_experts):
        mine = slice(l * expert_rows, (l + 1) * expert_rows)
        extra = slots[mine, model_width:].astype(jnp.float32)
        at = iota(extra.shape, 1) - 2 * experts_all
        low_rank = jnp.sum(
            jnp.where((at == seeds[l, 0]) | (at == factors + seeds[l, 0]), extra, 0.0),
            axis=1,
            keepdims=True,
        )
        right_row = jnp.sum(
            jnp.where(iota(table.shape, 0) == seeds[l, 1], table, 0.0), axis=0, keepdims=True
        )
        for n in range(steps):
            if first:
                copies[l * steps + n].wait()
            up_act = jnp.dot(
                slots[mine, :model_width],
                tiles[l * steps + n],
                preferred_element_type=jnp.float32,
            )
            here = slice(n * tile, (n + 1) * tile)
            up_act = jnp.maximum(up_act + low_rank * right_row[:, here], 0.0)
            hidden[l, :, here] = (up_act * up_act).astype(jnp.bfloat16)
    for copy in loads:
        copy.wait()


def down_kernel(parts, cores, pieces_out, *refs):
    pieces = refs[:parts]
    tiles, left, right, seeds_in, gate, own, *rest = refs[parts:]
    others, (results, left_in, right_in, seeds, sems) = rest[:-5], rest[-5:]
    local_experts, expert_rows, depth = pieces[0].shape
    steps = tiles.shape[0] // local_experts
    tile = tiles.shape[1]
    slot_count = local_experts * expert_rows
    tok_count = gate.shape[0] // cores

    tables = [
        pltpu.make_async_copy(left, left_in, sems.at[0]),
        pltpu.make_async_copy(right, right_in, sems.at[1]),
        pltpu.make_async_copy(seeds_in, seeds, sems.at[2]),
    ]
    for copy in tables:
        copy.start()

    columns = [slice(None)]
    if parts > 1:
        columns = [
            pl.ds(pl.multiple_of(lax.rem(my_part() - j + parts, parts) * depth, depth), depth)
            for j in range(parts)
        ]
    for copy in tables:
        copy.wait()
    for l in range(local_experts):
        rank_all = sum(
            lax.dot_general(left_in[:, at], piece[l], NT, preferred_element_type=jnp.float32)
            for at, piece in zip(columns, pieces)
        )
        rank = jnp.sum(
            jnp.where(iota(rank_all.shape, 0) == seeds[l, 2], rank_all, 0.0),
            axis=0,
            keepdims=True,
        )
        chosen = (iota((right.shape[0], expert_rows), 0) == seeds[l, 3]).astype(jnp.bfloat16)
        for n in range(steps):
            result = sum(
                lax.dot_general(
                    tiles[l * steps + n, :, at], piece[l], NT, preferred_element_type=jnp.float32
                )
                for at, piece in zip(columns, pieces)
            )
            here = slice(n * tile, (n + 1) * tile)
            right_column = lax.dot_general(
                right_in[:, here], chosen, TN, preferred_element_type=jnp.float32
            )
            result = (result + right_column * rank).astype(jnp.bfloat16)
            results[here, l * expert_rows : (l + 1) * expert_rows] = result
    summed = lax.dot_general(results[...], gate[...], NT, preferred_element_type=jnp.float32)
    own[...] = summed[:, :tok_count]
    step = summed.shape[0] // pieces_out
    for b in range(1, cores):
        for i in range(pieces_out):
            others[(b - 1) * pieces_out + i][...] = summed[
                i * step : (i + 1) * step, b * tok_count : (b + 1) * tok_count
            ].astype(jnp.bfloat16)


def on_device(
    tokens,
    routes,
    route_gates,
    up_weight,
    down_weight,
    factor_seeds,
    up_left,
    up_right,
    down_left,
    down_right,
):
    chips, cores, parts = lax.axis_size("ctx"), lax.axis_size("tp"), lax.axis_size("exp")
    local_experts, model_width, hid = up_weight.shape
    hid_all, out_width = down_weight.shape[1:]
    experts_all = chips * cores * local_experts
    tok_count, top_count = routes.shape
    factors = up_left.shape[0]
    capacity = 4 * tok_count * top_count // (3 * experts_all)
    rows = tok_count // parts
    width = -(-2 * (experts_all + factors) // LANES) * LANES
    packed = model_width + width
    expert_rows = cores * capacity
    slot_count = local_experts * expert_rows
    all_tokens = cores * tok_count
    whole_tiles = hid % LANES == 0
    params = pltpu.CompilerParams(vmem_limit_bytes=VMEM_LIMIT)
    vmem, hbm = (pl.BlockSpec(memory_space=space) for space in (pltpu.VMEM, pltpu.HBM))
    up_steps = 3 if hid % (3 * LANES) == 0 else 1
    up_tiles = (local_experts * up_steps, model_width, hid // up_steps)

    prep = pl.pallas_call(
        functools.partial(prep_kernel, experts_all, parts),
        out_shape=[jax.ShapeDtypeStruct((rows, packed), jnp.bfloat16)] * parts,
        in_specs=[hbm] * 4,
        out_specs=[vmem] * parts,
        scratch_shapes=[
            pltpu.VMEM((top_count, tok_count), jnp.int32),
            pltpu.VMEM((top_count, tok_count), jnp.float32),
            pltpu.VMEM(tokens.shape, jnp.bfloat16),
            pltpu.VMEM(up_left.shape, jnp.bfloat16),
            pltpu.VMEM((tok_count, width), jnp.bfloat16),
            pltpu.SemaphoreType.DMA((4,)),
        ],
        compiler_params=params,
        name="pack_tokens",
    )

    splits = 2 if rows % 32 == 0 else 1
    down_steps = 3 if out_width % 48 == 0 else 1
    down_tiles = (local_experts * down_steps, out_width // down_steps, hid_all)

    def up(first, load, count):
        return pl.pallas_call(
            functools.partial(
                up_kernel, first, load, count, rows, experts_all, parts, cores, capacity, factors
            ),
            out_shape=[
                jax.ShapeDtypeStruct((local_experts, expert_rows, hid), jnp.bfloat16),
                jax.ShapeDtypeStruct((all_tokens, slot_count), jnp.bfloat16),
            ]
            + [jax.ShapeDtypeStruct(up_tiles, jnp.bfloat16)] * first
            + [jax.ShapeDtypeStruct(down_tiles, jnp.bfloat16)] * load,
            in_specs=[vmem] * count
            + [hbm if first else vmem, hbm, hbm]
            + [hbm] * load,
            out_specs=[vmem] * (2 + first + load),
            scratch_shapes=[
                pltpu.VMEM((all_tokens, packed), jnp.bfloat16),
                pltpu.VMEM((slot_count, packed), jnp.bfloat16),
                pltpu.VMEM(up_right.shape, jnp.bfloat16),
                pltpu.SMEM(factor_seeds.shape, jnp.int32),
                pltpu.SemaphoreType.DMA((2 + up_tiles[0] + down_tiles[0],)),
            ],
            compiler_params=params,
            name="up",
        )

    r_splits = 2 if out_width % 64 == 0 else 1
    hidden_parts = parts if whole_tiles else 1

    down = pl.pallas_call(
        functools.partial(down_kernel, hidden_parts, cores, r_splits),
        out_shape=[jax.ShapeDtypeStruct((out_width, tok_count), jnp.float32)]
        + [jax.ShapeDtypeStruct((out_width // r_splits, tok_count), jnp.bfloat16)]
        * ((cores - 1) * r_splits),
        in_specs=[vmem] * (hidden_parts + 1) + [hbm, hbm, hbm, vmem],
        out_specs=[vmem] * (1 + (cores - 1) * r_splits),
        scratch_shapes=[
            pltpu.VMEM((out_width, slot_count), jnp.bfloat16),
            pltpu.VMEM(down_left.shape, jnp.bfloat16),
            pltpu.VMEM(down_right.shape, jnp.bfloat16),
            pltpu.SMEM(factor_seeds.shape, jnp.int32),
            pltpu.SemaphoreType.DMA((3,)),
        ],
        compiler_params=params,
        name="down",
    )

    in_hbm = [
        in_memory(value, pltpu.HBM)
        for value in (
            routes.T, route_gates.T, tokens, up_left, up_weight, up_right,
            down_weight.transpose(0, 2, 1), down_left, down_right, factor_seeds,
        )
    ]
    up_weight, up_right, down_turned, down_left, down_right, seeds = in_hbm[4:]
    pieces = list(prep(*in_hbm[:4]))
    kept = {}

    last = [pieces[0]]

    def order(value):
        last[0] = after(value, last[0])
        return last[0]

    def halves_of(piece):
        step = rows // splits
        return [piece[i * step : (i + 1) * step] for i in range(splits)]

    def over_cores(halves):
        return [[shift(half, "tp", b) for half in halves] for b in range(1, cores)]

    def over_exp(value):
        return [shift(value, "exp", j) for j in range(1, parts)]

    def up_only(here, there, load=False):
        blocks = [half for halves in here for half in halves]
        for b in range(cores - 1):
            blocks += [half for others in there for half in others[b]]
        first = "up" not in kept
        hidden, gate, *tiles = up(first, load, len(blocks))(
            order(blocks[0]),
            *blocks[1:],
            up_weight if first else kept["up"],
            up_right,
            seeds,
            *([down_turned] if load else []),
        )
        if load:
            kept["down"] = tiles.pop()
        if first:
            kept["up"] = tiles[0]
        last[0] = gate
        return hidden, gate

    def exchanged(hidden):
        if whole_tiles:
            return [hidden] + over_exp(hidden)
        return [lax.all_gather(hidden, "exp", axis=2, tiled=True)]

    def run_down(hiddens, gate):
        own, *others = down(
            *hiddens[:-1],
            order(hiddens[-1]),
            kept["down"],
            down_left,
            down_right,
            seeds,
            gate,
        )
        last[0] = own
        return own, others

    def back(others):
        return [
            [shift(others[(b - 1) * r_splits + i], "tp", -b) for i in range(r_splits)]
            for b in range(1, cores)
        ]

    def add(own, swapped, *values):
        arrays = [piece for pieces in swapped for piece in pieces]

        def kernel(own, *refs):
            out, refs = refs[-1], refs[:-1]
            step = own.shape[0] // r_splits
            for i in range(r_splits):
                at = slice(i * step, (i + 1) * step)
                total = own[at, :]
                for b in range(cores - 1):
                    total = total + refs[b * r_splits + i][...].astype(jnp.float32)
                for value in refs[len(arrays) :]:
                    total = total + value[at, :].astype(jnp.float32)
                out[at, :] = total.astype(jnp.bfloat16)

        return pl.pallas_call(
            kernel,
            out_shape=jax.ShapeDtypeStruct(own.shape, jnp.bfloat16),
            in_specs=[vmem] * (1 + len(arrays) + len(values)),
            out_specs=vmem,
            compiler_params=params,
            cost_estimate=pl.CostEstimate(flops=1, bytes_accessed=1, transcendentals=0),
            name="add",
        )(own, *arrays, *values)

    def summed(own, others, *more):
        return add(own, back(others), *more)

    returned = {}

    def give_back(k, own, others):
        total = order(
            summed(own, [after(others[0], last[0])] + others[1:], *([returned[k - 1]] if k > 2 else []))
        )
        returned[k] = shift(total, "ctx", -1 if k == 1 else 1)

    def send_direct(earlier):
        return [shift(after(piece, earlier), "ctx", -1) for piece in pieces[1:]]

    arriving = shift(pieces[0], "ctx", 1)
    direct = [halves_of(piece) for piece in pieces[1:]]
    direct = [[shift(halves[0], "ctx", -1)] + halves[1:] for halves in direct]
    hidden_own, gate_own = up_only(
        [[piece] for piece in pieces],
        [over_cores(halves_of(piece)) for piece in pieces],
        load=True,
    )
    arriving = order(arriving)
    direct = [[order(halves[0])] + halves[1:] for halves in direct]
    mine_there = over_cores(halves_of(arriving))
    work = [None]
    for k in range(1, chips):
        if k == max(1, chips - 2):
            direct = [
                halves[:1] + [shift(after(half, arriving), "ctx", -1) for half in halves[1:]]
                for halves in direct
            ]
        if k < chips - 1:
            here = [[piece] for piece in [arriving] + over_exp(arriving)]
        else:
            here = [[arriving]] + direct
        there = [mine_there]
        if k < chips - 1:
            arriving = shift(arriving, "ctx", 1)
        if k == 1:
            arriving = order(arriving)
        here[1:] = [halves[:-1] + [order(halves[-1])] for halves in here[1:]]
        there += [
            over_cores(halves_of(halves[0]) if len(halves) == 1 else halves) for halves in here[1:]
        ]
        if k < chips - 2:
            mine_there = over_cores(halves_of(arriving))
        hidden, gate = up_only(here, there)
        work.append((exchanged(hidden), gate))
        if 1 < k < chips - 1:
            arriving = order(arriving)
            if k == chips - 2:
                mine_there = over_cores(halves_of(arriving))
    hidden_own = after(hidden_own, gate)
    work[0] = (exchanged(hidden_own), gate_own)
    for k in range(1, chips):
        sums = run_down(*work[k])
        give_back(k, *sums)
        if 1 < k == chips - 2:
            returned[1] = order(returned[1])
    own_sum, own_others = run_down(*work[0])
    homeward = {1, chips - 1}
    return add(own_sum, back(own_others), *(returned[k] for k in sorted(homeward))).T


def solution(mesh):
    in_specs = (
        P(("pop", "ctx", "tp"), None),
        P(("pop", "ctx", "tp"), None),
        P(("pop", "ctx", "tp"), None),
        P(("ctx", "tp"), None, "exp"),
        P(("ctx", "tp"), None, "exp"),
        P(("pop", "ctx", "tp"), None),
        P(),
        P(None, "exp"),
        P(),
        P(None, "exp"),
    )
    out_specs = P(("pop", "ctx", "tp"), "exp")
    return jax.shard_map(
        on_device, mesh=mesh, in_specs=in_specs, out_specs=out_specs, check_vma=False
    )
```

```python
import functools

import jax
import jax.numpy as jnp
from jax import lax
from jax.experimental import pallas as pl
from jax.experimental.pallas import tpu as pltpu
from jax.sharding import PartitionSpec as P

LANES = 128
VMEM_LIMIT = 24 * 1024 * 1024
NT = (((1,), (1,)), ((), ()))
TN = (((0,), (0,)), ((), ()))


def shift(value, axis, by):
    size = lax.axis_size(axis)
    return lax.ppermute(value, axis, [(i, (i + by) % size) for i in range(size)])


in_memory = pltpu.with_memory_space_constraint


def after(value, earlier):
    return lax.optimization_barrier((value, earlier))[0]


def iota(shape, dim):
    return lax.broadcasted_iota(jnp.int32, shape, dim)


def my_part():
    return lax.axis_index("exp")


def first_expert(local_experts):
    return (lax.axis_index("ctx") * lax.axis_size("tp") + lax.axis_index("tp")) * local_experts


def prep_kernel(experts_all, parts, routes, gates, tokens, up_left, *refs):
    pieces, (routes_in, gates_in, rows_in, table_in, info, sems) = refs[:parts], refs[parts:]
    count, model_width = tokens.shape
    width = info.shape[1]
    factors = up_left.shape[0]
    rows = count // parts
    copies = [
        pltpu.make_async_copy(source, target, sems.at[i])
        for i, (source, target) in enumerate(
            ((routes, routes_in), (gates, gates_in), (up_left, table_in), (tokens, rows_in))
        )
    ]
    for copy in copies:
        copy.start()
    line = iota((width, count), 0)
    expert = lax.rem(line, experts_all)
    after_it = (iota((count, count), 0) < iota((count, count), 1)).astype(jnp.bfloat16)
    row = iota((width, factors), 0) - 2 * experts_all
    pick = (row >= 0) & (row < 2 * factors) & (lax.rem(row, factors) == iota((width, factors), 1))
    for copy in copies[:2]:
        copy.wait()
    gate_all = gates_in[...]
    normed = gate_all / jnp.sum(gate_all, axis=0, keepdims=True)
    named = jnp.zeros((width, count), jnp.float32)
    gate = jnp.zeros((width, count), jnp.float32)
    for k in range(routes.shape[0]):
        hit = routes_in[k : k + 1, :] == expert
        named = jnp.where(hit, 1.0, named)
        gate = jnp.where(hit, normed[k : k + 1, :], gate)
    slot = jnp.dot(named.astype(jnp.bfloat16), after_it, preferred_element_type=jnp.float32)
    slot = jnp.where(named > 0.0, slot, -1.0)
    copies[2].wait()
    left = jnp.dot(
        pick.astype(jnp.bfloat16), table_in[...], preferred_element_type=jnp.float32
    ).astype(jnp.bfloat16)
    copies[3].wait()
    low_rank = lax.dot_general(left, rows_in[...], NT, preferred_element_type=jnp.float32)
    value = jnp.where(line < 2 * experts_all, gate, low_rank)
    high = value.astype(jnp.bfloat16).astype(jnp.float32)
    is_low = line >= 2 * experts_all + factors
    value = jnp.where(is_low, value - high, high)
    info[...] = jnp.where(line < experts_all, slot, value).T.astype(jnp.bfloat16)
    for j, piece in enumerate(pieces):
        at = pl.multiple_of(lax.rem(my_part() - j + parts, parts) * rows, rows)
        piece[:, :model_width] = rows_in[pl.ds(at, rows), :]
        piece[:, model_width:] = info[pl.ds(at, rows), :]


def up_kernel(first, load, count, rows, experts_all, parts, cores, capacity, factors, *refs):
    pieces = refs[:count]
    weight, right, seeds_in, *rest = refs[count:-5]
    down_weight = rest.pop(0) if load else None
    hidden, gate_out, *tiles = rest
    down_tiles = tiles.pop() if load else None
    block, slots, right_in, seeds, sems = refs[-5:]
    tok_count = rows * parts
    tiles = tiles[0] if first else weight
    local_experts, _, hid = hidden.shape
    steps = tiles.shape[0] // local_experts
    model_width, tile = tiles.shape[1:]
    width = block.shape[1] - model_width
    expert_rows = cores * capacity
    slot_count = local_experts * expert_rows

    tables = [
        pltpu.make_async_copy(right, right_in, sems.at[0]),
        pltpu.make_async_copy(seeds_in, seeds, sems.at[1]),
    ]
    copies = []
    if first:
        copies = [
            pltpu.make_async_copy(
                weight.at[l, :, pl.ds(n * tile, tile)],
                tiles.at[l * steps + n],
                sems.at[2 + l * steps + n],
            )
            for l in range(local_experts)
            for n in range(steps)
        ]
    loads = []
    if load:
        down_steps = down_tiles.shape[0] // local_experts
        down_tile = down_tiles.shape[1]
        loads = [
            pltpu.make_async_copy(
                down_weight.at[l, pl.ds(n * down_tile, down_tile), :],
                down_tiles.at[l * down_steps + n],
                sems.at[2 + len(copies) + l * down_steps + n],
            )
            for l in range(local_experts)
            for n in range(down_steps)
        ]
    for copy in tables + copies + loads:
        copy.start()

    column = iota((width, slot_count), 0)
    slot = iota((width, slot_count), 1)
    owner = first_expert(local_experts) + slot // expert_rows
    place_of = (column == owner).astype(jnp.bfloat16)
    gate_of = (column == owner + experts_all).astype(jnp.bfloat16)
    lane = iota((cores * tok_count, slot_count), 1)
    wanted = lax.rem(lane, capacity).astype(jnp.float32)
    same_core = lax.rem(lane, expert_rows) // capacity == iota(lane.shape, 0) // tok_count
    base = 0
    for piece in pieces:
        block[base : base + piece.shape[0], :] = piece[...]
        base += piece.shape[0]
    info = block[:, model_width:]
    slot_of = jnp.dot(info, place_of, preferred_element_type=jnp.float32)
    here = (slot_of == wanted) & same_core
    slots[...] = lax.dot_general(
        here.astype(jnp.bfloat16), block[...], TN, preferred_element_type=jnp.float32
    ).astype(jnp.bfloat16)
    gate = jnp.dot(info, gate_of, preferred_element_type=jnp.float32)
    gate = jnp.where(here, gate, 0.0).astype(jnp.bfloat16)
    for b in range(cores):
        for j in range(parts):
            base = b * tok_count + j * rows
            at = b * tok_count + lax.rem(my_part() - j + parts, parts) * rows
            gate_out[pl.ds(pl.multiple_of(at, rows), rows), :] = gate[base : base + rows, :]

    for copy in tables:
        copy.wait()
    table = right_in[...].astype(jnp.float32)
    for l in range(local_experts):
        mine = slice(l * expert_rows, (l + 1) * expert_rows)
        extra = slots[mine, model_width:].astype(jnp.float32)
        at = iota(extra.shape, 1) - 2 * experts_all
        low_rank = jnp.sum(
            jnp.where((at == seeds[l, 0]) | (at == factors + seeds[l, 0]), extra, 0.0),
            axis=1,
            keepdims=True,
        )
        right_row = jnp.sum(
            jnp.where(iota(table.shape, 0) == seeds[l, 1], table, 0.0), axis=0, keepdims=True
        )
        for n in range(steps):
            if first:
                copies[l * steps + n].wait()
            up_act = jnp.dot(
                slots[mine, :model_width],
                tiles[l * steps + n],
                preferred_element_type=jnp.float32,
            )
            here = slice(n * tile, (n + 1) * tile)
            up_act = jnp.maximum(up_act + low_rank * right_row[:, here], 0.0)
            hidden[l, :, here] = (up_act * up_act).astype(jnp.bfloat16)
    for copy in loads:
        copy.wait()


def down_kernel(parts, cores, pieces_out, *refs):
    pieces = refs[:parts]
    tiles, left, right, seeds_in, gate, own, *rest = refs[parts:]
    others, (results, left_in, right_in, seeds, sems) = rest[:-5], rest[-5:]
    local_experts, expert_rows, depth = pieces[0].shape
    steps = tiles.shape[0] // local_experts
    tile = tiles.shape[1]
    slot_count = local_experts * expert_rows
    tok_count = gate.shape[0] // cores

    tables = [
        pltpu.make_async_copy(left, left_in, sems.at[0]),
        pltpu.make_async_copy(right, right_in, sems.at[1]),
        pltpu.make_async_copy(seeds_in, seeds, sems.at[2]),
    ]
    for copy in tables:
        copy.start()

    columns = [slice(None)]
    if parts > 1:
        columns = [
            pl.ds(pl.multiple_of(lax.rem(my_part() - j + parts, parts) * depth, depth), depth)
            for j in range(parts)
        ]
    for copy in tables:
        copy.wait()
    for l in range(local_experts):
        rank_all = sum(
            lax.dot_general(left_in[:, at], piece[l], NT, preferred_element_type=jnp.float32)
            for at, piece in zip(columns, pieces)
        )
        rank = jnp.sum(
            jnp.where(iota(rank_all.shape, 0) == seeds[l, 2], rank_all, 0.0),
            axis=0,
            keepdims=True,
        )
        chosen = (iota((right.shape[0], expert_rows), 0) == seeds[l, 3]).astype(jnp.bfloat16)
        for n in range(steps):
            result = sum(
                lax.dot_general(
                    tiles[l * steps + n, :, at], piece[l], NT, preferred_element_type=jnp.float32
                )
                for at, piece in zip(columns, pieces)
            )
            here = slice(n * tile, (n + 1) * tile)
            right_column = lax.dot_general(
                right_in[:, here], chosen, TN, preferred_element_type=jnp.float32
            )
            result = (result + right_column * rank).astype(jnp.bfloat16)
            results[here, l * expert_rows : (l + 1) * expert_rows] = result
    summed = lax.dot_general(results[...], gate[...], NT, preferred_element_type=jnp.float32)
    own[...] = summed[:, :tok_count]
    step = summed.shape[0] // pieces_out
    for b in range(1, cores):
        for i in range(pieces_out):
            others[(b - 1) * pieces_out + i][...] = summed[
                i * step : (i + 1) * step, b * tok_count : (b + 1) * tok_count
            ].astype(jnp.bfloat16)


def on_device(
    tokens,
    routes,
    route_gates,
    up_weight,
    down_weight,
    factor_seeds,
    up_left,
    up_right,
    down_left,
    down_right,
):
    chips, cores, parts = lax.axis_size("ctx"), lax.axis_size("tp"), lax.axis_size("exp")
    local_experts, model_width, hid = up_weight.shape
    hid_all, out_width = down_weight.shape[1:]
    experts_all = chips * cores * local_experts
    tok_count, top_count = routes.shape
    factors = up_left.shape[0]
    capacity = 4 * tok_count * top_count // (3 * experts_all)
    rows = tok_count // parts
    width = -(-2 * (experts_all + factors) // LANES) * LANES
    packed = model_width + width
    expert_rows = cores * capacity
    slot_count = local_experts * expert_rows
    all_tokens = cores * tok_count
    whole_tiles = hid % LANES == 0
    params = pltpu.CompilerParams(vmem_limit_bytes=VMEM_LIMIT)
    vmem, hbm = (pl.BlockSpec(memory_space=space) for space in (pltpu.VMEM, pltpu.HBM))
    up_steps = 3 if hid % (3 * LANES) == 0 else 1
    up_tiles = (local_experts * up_steps, model_width, hid // up_steps)

    prep = pl.pallas_call(
        functools.partial(prep_kernel, experts_all, parts),
        out_shape=[jax.ShapeDtypeStruct((rows, packed), jnp.bfloat16)] * parts,
        in_specs=[hbm] * 4,
        out_specs=[vmem] * parts,
        scratch_shapes=[
            pltpu.VMEM((top_count, tok_count), jnp.int32),
            pltpu.VMEM((top_count, tok_count), jnp.float32),
            pltpu.VMEM(tokens.shape, jnp.bfloat16),
            pltpu.VMEM(up_left.shape, jnp.bfloat16),
            pltpu.VMEM((tok_count, width), jnp.bfloat16),
            pltpu.SemaphoreType.DMA((4,)),
        ],
        compiler_params=params,
        name="pack_tokens",
    )

    splits = 2 if rows % 32 == 0 else 1
    down_steps = 3 if out_width % 48 == 0 else 1
    down_tiles = (local_experts * down_steps, out_width // down_steps, hid_all)

    def up(first, load, count):
        return pl.pallas_call(
            functools.partial(
                up_kernel, first, load, count, rows, experts_all, parts, cores, capacity, factors
            ),
            out_shape=[
                jax.ShapeDtypeStruct((local_experts, expert_rows, hid), jnp.bfloat16),
                jax.ShapeDtypeStruct((all_tokens, slot_count), jnp.bfloat16),
            ]
            + [jax.ShapeDtypeStruct(up_tiles, jnp.bfloat16)] * first
            + [jax.ShapeDtypeStruct(down_tiles, jnp.bfloat16)] * load,
            in_specs=[vmem] * count
            + [hbm if first else vmem, hbm, hbm]
            + [hbm] * load,
            out_specs=[vmem] * (2 + first + load),
            scratch_shapes=[
                pltpu.VMEM((all_tokens, packed), jnp.bfloat16),
                pltpu.VMEM((slot_count, packed), jnp.bfloat16),
                pltpu.VMEM(up_right.shape, jnp.bfloat16),
                pltpu.SMEM(factor_seeds.shape, jnp.int32),
                pltpu.SemaphoreType.DMA((2 + up_tiles[0] + down_tiles[0],)),
            ],
            compiler_params=params,
            name="up",
        )

    r_splits = 2 if out_width % 64 == 0 else 1
    hidden_parts = parts if whole_tiles else 1

    down = pl.pallas_call(
        functools.partial(down_kernel, hidden_parts, cores, r_splits),
        out_shape=[jax.ShapeDtypeStruct((out_width, tok_count), jnp.float32)]
        + [jax.ShapeDtypeStruct((out_width // r_splits, tok_count), jnp.bfloat16)]
        * ((cores - 1) * r_splits),
        in_specs=[vmem] * (hidden_parts + 1) + [hbm, hbm, hbm, vmem],
        out_specs=[vmem] * (1 + (cores - 1) * r_splits),
        scratch_shapes=[
            pltpu.VMEM((out_width, slot_count), jnp.bfloat16),
            pltpu.VMEM(down_left.shape, jnp.bfloat16),
            pltpu.VMEM(down_right.shape, jnp.bfloat16),
            pltpu.SMEM(factor_seeds.shape, jnp.int32),
            pltpu.SemaphoreType.DMA((3,)),
        ],
        compiler_params=params,
        name="down",
    )

    in_hbm = [
        in_memory(value, pltpu.HBM)
        for value in (
            routes.T, route_gates.T, tokens, up_left, up_weight, up_right,
            down_weight.transpose(0, 2, 1), down_left, down_right, factor_seeds,
        )
    ]
    up_weight, up_right, down_turned, down_left, down_right, seeds = in_hbm[4:]
    pieces = list(prep(*in_hbm[:4]))
    kept = {}

    last = [pieces[0]]

    def order(value):
        last[0] = after(value, last[0])
        return last[0]

    def halves_of(piece):
        step = rows // splits
        return [piece[i * step : (i + 1) * step] for i in range(splits)]

    def over_cores(halves):
        return [[shift(half, "tp", b) for half in halves] for b in range(1, cores)]

    def over_exp(value):
        return [shift(value, "exp", j) for j in range(1, parts)]

    def up_only(here, there, load=False):
        blocks = [half for halves in here for half in halves]
        for b in range(cores - 1):
            blocks += [half for others in there for half in others[b]]
        first = "up" not in kept
        hidden, gate, *tiles = up(first, load, len(blocks))(
            order(blocks[0]),
            *blocks[1:],
            up_weight if first else kept["up"],
            up_right,
            seeds,
            *([down_turned] if load else []),
        )
        if load:
            kept["down"] = tiles.pop()
        if first:
            kept["up"] = tiles[0]
        last[0] = gate
        return hidden, gate

    def exchanged(hidden):
        if whole_tiles:
            return [hidden] + over_exp(hidden)
        return [lax.all_gather(hidden, "exp", axis=2, tiled=True)]

    def run_down(hiddens, gate):
        own, *others = down(
            *hiddens[:-1],
            order(hiddens[-1]),
            kept["down"],
            down_left,
            down_right,
            seeds,
            gate,
        )
        last[0] = own
        return own, others

    def back(others):
        return [
            [shift(others[(b - 1) * r_splits + i], "tp", -b) for i in range(r_splits)]
            for b in range(1, cores)
        ]

    def add(own, swapped, *values):
        arrays = [piece for pieces in swapped for piece in pieces]

        def kernel(own, *refs):
            out, refs = refs[-1], refs[:-1]
            step = own.shape[0] // r_splits
            for i in range(r_splits):
                at = slice(i * step, (i + 1) * step)
                total = own[at, :]
                for b in range(cores - 1):
                    total = total + refs[b * r_splits + i][...].astype(jnp.float32)
                for value in refs[len(arrays) :]:
                    total = total + value[at, :].astype(jnp.float32)
                out[at, :] = total.astype(jnp.bfloat16)

        return pl.pallas_call(
            kernel,
            out_shape=jax.ShapeDtypeStruct(own.shape, jnp.bfloat16),
            in_specs=[vmem] * (1 + len(arrays) + len(values)),
            out_specs=vmem,
            compiler_params=params,
            cost_estimate=pl.CostEstimate(flops=1, bytes_accessed=1, transcendentals=0),
            name="add",
        )(own, *arrays, *values)

    def summed(own, others, *more):
        return add(own, back(others), *more)

    returned = {}

    def give_back(k, own, others):
        total = order(
            summed(own, [after(others[0], last[0])] + others[1:], *([returned[k - 1]] if k > 2 else []))
        )
        returned[k] = shift(total, "ctx", -1 if k == 1 else 1)

    def send_direct(earlier):
        return [shift(after(piece, earlier), "ctx", -1) for piece in pieces[1:]]

    arriving = shift(pieces[0], "ctx", 1)
    direct = [halves_of(piece) for piece in pieces[1:]]
    direct = [[shift(halves[0], "ctx", -1)] + halves[1:] for halves in direct]
    hidden_own, gate_own = up_only(
        [[piece] for piece in pieces],
        [over_cores(halves_of(piece)) for piece in pieces],
        load=True,
    )
    arriving = order(arriving)
    direct = [[order(halves[0])] + halves[1:] for halves in direct]
    mine_there = over_cores(halves_of(arriving))
    work = [None]
    for k in range(1, chips):
        if k == max(1, chips - 2):
            direct = [
                halves[:1] + [shift(after(half, arriving), "ctx", -1) for half in halves[1:]]
                for halves in direct
            ]
        if k < chips - 1:
            here = [[piece] for piece in [arriving] + over_exp(arriving)]
        else:
            here = [[arriving]] + direct
        there = [mine_there]
        if k < chips - 1:
            arriving = shift(arriving, "ctx", 1)
        if k == 1:
            arriving = order(arriving)
        here[1:] = [halves[:-1] + [order(halves[-1])] for halves in here[1:]]
        there += [
            over_cores(halves_of(halves[0]) if len(halves) == 1 else halves) for halves in here[1:]
        ]
        if k < chips - 2:
            mine_there = over_cores(halves_of(arriving))
        hidden, gate = up_only(here, there)
        work.append((exchanged(hidden), gate))
        if 1 < k < chips - 1:
            arriving = order(arriving)
            if k == chips - 2:
                mine_there = over_cores(halves_of(arriving))
    hidden_own = after(hidden_own, gate)
    work[0] = (exchanged(hidden_own), gate_own)
    for k in range(1, chips):
        sums = run_down(*work[k])
        give_back(k, *sums)
        if 1 < k == chips - 2:
            returned[1] = order(returned[1])
    own_sum, own_others = run_down(*work[0])
    homeward = {1, chips - 1}
    return add(own_sum, back(own_others), *(returned[k] for k in sorted(homeward))).T


def solution(mesh):
    in_specs = (
        P(("pop", "ctx", "tp"), None),
        P(("pop", "ctx", "tp"), None),
        P(("pop", "ctx", "tp"), None),
        P(("ctx", "tp"), None, "exp"),
        P(("ctx", "tp"), None, "exp"),
        P(("pop", "ctx", "tp"), None),
        P(),
        P(None, "exp"),
        P(),
        P(None, "exp"),
    )
    out_specs = P(("pop", "ctx", "tp"), "exp")
    return jax.shard_map(
        on_device, mesh=mesh, in_specs=in_specs, out_specs=out_specs, check_vma=False
    )
```
